256 devices in a mesh: ta: 8 (over x, z_hi), tp: 32 (over y, z_lo, core).
Axes of the slice: x: 4, y: 4, z: 8 (z_hi: 2, z_lo: 4; z = z_hi * 4 + z_lo), core: 2. Of those that a mesh axis runs over, the one named last changes fastest.
Arguments:
- green: float32 [2, 8, 32, 16, 4096], P(None, None, 'tp', None, 'ta'), may hold values from -5 to 5
- hamiltonian: float32 [32, 32], replicated, may hold values from -1 to 1
- interaction: float32 [32, 32], replicated, may hold values from 0.4 to 1.2
Outputs:
- green_next: float32 [2, 8, 32, 16, 4096], P(None, None, 'tp', None, 'ta')
The draws below stay inside these ranges and needn't reach their ends.
All inputs are finite; a program needn't handle non-finite values.
Results may differ from the reference program's by a relative error of at most 0.0091.
Values may be sent and summed in bfloat16 or wider, within the bound.
A program may use at most 64 MiB of HBM per device.

```python
import math
import jax
import jax.numpy as jnp
from jax import lax

NO = 32
W = 16
ITERS = 2
ORDER = 4096
MEMT = 32
N_TA = 8
N_TP = 32


def level_of(own_key, dims, pieces, low, largest):
    factor_of = 1.0
    for dim, blocks in pieces:
        steps = jax.random.uniform(jax.random.fold_in(jax.random.fold_in(own_key, 6), dim), (blocks,), jnp.float32, low / len(pieces), largest / len(pieces))
        factor_of = factor_of * jnp.repeat(jnp.exp(steps), dims[dim] // blocks).reshape((-1,) + (1,) * (len(dims) - 1 - dim))
    return factor_of


def centred(rng, shape, width, reach, pieces=(), held_as=jnp.bfloat16):
    entries = width * jax.random.normal(rng, shape, jnp.float32)
    if pieces:
        entries = entries * level_of(rng, shape, pieces, -0.22, 0.18)
    return jnp.clip(entries, -reach, reach).astype(held_as)


def setup_inputs(seed: int = 0) -> dict:
    streams_of = jax.random.split(jax.random.key(seed), 4)
    green = centred(streams_of[0], (2, N_TA, N_TP, W, ORDER), 0.7, 5.0, ((2, 32), (4, 8)), jnp.float32)
    hamiltonian = centred(streams_of[1], (NO, NO), NO ** -0.5, 1.0, (), jnp.float32)
    interaction = jnp.clip(jnp.exp(jax.random.uniform(streams_of[2], (NO, NO), jnp.float32, math.log(0.4), math.log(1.2))), 0.4, 1.2)
    return dict(green=green, hamiltonian=hamiltonian, interaction=interaction)


highest = lax.Precision.HIGHEST

def real_dot(left_side, right_side):
    return jnp.dot(left_side, right_side, precision=highest, preferred_element_type=jnp.float32)

def reference(green, hamiltonian, interaction):
    full_order = N_TA * N_TP * W
    block_rows = N_TP * W
    time_count = full_order // NO
    factor = 1.0 / math.sqrt(MEMT * NO)
    current = green.reshape(2, full_order, full_order)
    coupling = (interaction * interaction).T.reshape(1, NO, 1, NO)
    row_time = jnp.arange(full_order, dtype=jnp.int32) // NO
    inside = (row_time[:, None] <= row_time[None, :]) & (row_time[:, None] > row_time[None, :] - MEMT)
    padding = 2 * block_rows
    for iteration in range(ITERS):
        rounded = current.astype(jnp.bfloat16)
        lowered = lax.optimization_barrier(rounded).astype(jnp.float32)
        mirrored = jnp.swapaxes(lowered, 1, 2)
        real_square = current[0] * current[0] - current[1] * current[1]
        imag_square = 2.0 * current[0] * current[1]
        sigma_real = real_square * mirrored[0] - imag_square * mirrored[1]
        sigma_imag = real_square * mirrored[1] + imag_square * mirrored[0]
        sigma = jnp.stack([sigma_real, sigma_imag]).reshape(2, time_count, NO, time_count, NO) * coupling
        sigma = jnp.where(inside, sigma.reshape(2, full_order, full_order), 0.0)
        window = sigma.astype(jnp.bfloat16)
        window_low = lax.optimization_barrier(window).astype(jnp.float32)
        padded_green = jnp.pad(lowered, ((0, 0), (0, 0), (padding, 0)))
        padded_sigma = jnp.pad(window_low, ((0, 0), (padding, 0), (0, 0)))

        def one_block(block_index):
            begin_at = block_index * block_rows
            left_side = lax.dynamic_slice_in_dim(padded_green, begin_at, 3 * block_rows, 2)
            right_side = lax.dynamic_slice_in_dim(padded_sigma, begin_at, 3 * block_rows, 1)
            right_side = lax.dynamic_slice_in_dim(right_side, begin_at, block_rows, 2)
            product_real = real_dot(left_side[0], right_side[0]) - real_dot(left_side[1], right_side[1])
            product_imag = real_dot(left_side[0], right_side[1]) + real_dot(left_side[1], right_side[0])
            return jnp.stack([product_real, product_imag])
        block_results = lax.map(one_block, jnp.arange(N_TA, dtype=jnp.int32))
        memory = jnp.transpose(block_results, (1, 2, 0, 3)).reshape(2, full_order, full_order)
        hamilton_term = jnp.einsum('pxtk,ik->pxti', current.reshape(2, full_order, time_count, NO), hamiltonian, precision=highest).reshape(2, full_order, full_order)
        next_real = current[0] + 0.5 * (hamilton_term[1] + factor * memory[1])
        next_imag = current[1] - 0.5 * (hamilton_term[0] + factor * memory[0])
        current = jnp.stack([next_real, next_imag])
    return current.reshape(2, N_TA, N_TP, W, full_order)
```

```python
import functools

import jax
import jax.numpy as jnp
from jax import lax
from jax.experimental import pallas as pl
from jax.experimental.pallas import tpu as pltpu
from jax.sharding import PartitionSpec as P

NO = 32
ITERS = 2
N_TA = 8
N_TP = 32
N_Y = 4
N_Z = 4
STRIPE = 16
ROWS = 512
COLS = 128
FACTOR = 1.0 / 32.0

MESH = pl.DeviceIdType.MESH
HIGHEST = lax.Precision.HIGHEST
F32 = jnp.float32
BF16 = jnp.bfloat16


def iota(shape, dim):
    return lax.broadcasted_iota(jnp.int32, shape, dim)


def exact_dot(left, right, contract=((1,), (0,))):
    return lax.dot_general(
        left, right, (contract, ((), ())), precision=HIGHEST, preferred_element_type=F32
    )


def kernel(
    green_ref,
    ham_ref,
    inter_ref,
    out_ref,
    rounded,
    previous,
    earliest,
    mirror_out,
    mirror_in,
    flip_own,
    flip_out,
    flip_in,
    window,
    straight,
    crossed,
    total,
    hamilton,
    weights,
    blocked,
    row_send,
    row_recv,
    mirror_send,
    mirror_recv,
    flip_send,
    flip_recv,
    window_send,
    window_recv,
):
    ta = lax.axis_index("ta")
    tp = lax.axis_index("tp")
    y = tp // 8
    zl = lax.rem(tp // 2, 4)
    core = lax.rem(tp, 2)

    def ta_plus(k):
        return lax.rem(ta + k + N_TA, N_TA)

    def place(dy, z, c):
        return lax.rem(y + dy, N_Y) * 8 + z * 2 + c

    barrier = pltpu.get_barrier_semaphore()

    def greet(k, carry):
        pl.semaphore_signal(
            barrier, inc=1, device_id=(ta, lax.rem(tp + k, N_TP)), device_id_type=MESH
        )
        return carry

    lax.fori_loop(1, N_TP, greet, 0)
    for k in (1, 2):
        pl.semaphore_signal(
            barrier, inc=1, device_id=(ta_plus(-k), tp), device_id_type=MESH
        )

    def remote(src, dst, send, recv, target):
        return pltpu.make_async_remote_copy(
            src_ref=src,
            dst_ref=dst,
            send_sem=send,
            recv_sem=recv,
            device_id=target,
            device_id_type=MESH,
        )

    def build_mirror(state, it):
        pieces = []
        for k in range(3):
            group = pl.multiple_of(ta_plus(k) * STRIPE, STRIPE)
            for r in range(2):
                pieces.append(state[r, pl.ds(group, STRIPE), :])
        pieces.append(jnp.zeros((2 * STRIPE, ROWS), F32))
        stacked = jnp.concatenate(pieces, axis=0)
        mirror_out[it] = stacked.T.astype(BF16)

    def build_rounded(state, it):
        for r in range(2):
            rounded[it, pl.ds(r * COLS, COLS), :] = state[r].astype(BF16)

    def row_copy(it, k):
        return remote(
            rounded.at[it],
            (previous if k == 1 else earliest).at[it],
            row_send.at[it, k - 1],
            row_recv.at[it, k - 1],
            (ta_plus(k), tp),
        )

    def flip_copy(it, k):
        return remote(
            flip_out.at[it, k - 1],
            flip_in.at[it, k - 1],
            flip_send.at[it, k - 1],
            flip_recv.at[it, k - 1],
            (ta_plus(k), tp),
        )

    def send_mirror(it):
        def send(k, carry):
            peer = lax.rem(tp + k, N_TP)
            remote(
                mirror_out.at[it, pl.ds(pl.multiple_of(peer * STRIPE, STRIPE), STRIPE), :],
                mirror_in.at[it, pl.ds(pl.multiple_of(tp * STRIPE, STRIPE), STRIPE), :],
                mirror_send.at[it],
                mirror_recv.at[it],
                (ta, peer),
            ).start()
            return carry

        lax.fori_loop(1, N_TP, send, 0)
        own = pl.ds(pl.multiple_of(tp * STRIPE, STRIPE), STRIPE)
        mirror_in[it, own, :] = mirror_out[it, own, :]

    def wait_bytes(ref, sem):
        pltpu.make_async_copy(ref, ref, sem).wait()

    def flip(it):
        piece = iota((STRIPE, 128), 1) // STRIPE
        for j in range(4):
            parts = [
                mirror_in[it, pl.ds((j * 8 + i) * STRIPE, STRIPE), :].astype(F32)
                for i in range(8)
            ]
            for bit in (1, 2, 4):
                low = (piece // bit) % 2 == 0
                for i in range(8):
                    if i & bit:
                        continue
                    first, second = parts[i], parts[i | bit]
                    parts[i] = jnp.where(low, first, pltpu.roll(second, STRIPE * bit, 1))
                    parts[i | bit] = jnp.where(
                        low, pltpu.roll(first, 128 - STRIPE * bit, 1), second
                    )
            for k in range(3):
                both = jnp.concatenate([parts[2 * k], parts[2 * k + 1]], axis=0).astype(BF16)
                lanes = pl.ds(j * 128, 128)
                if k == 0:
                    flip_own[:, lanes] = both
                else:
                    flip_out[it, k - 1, :, lanes] = both

    def column(state, r, k):
        group = pl.multiple_of(ta_plus(-k) * STRIPE, STRIPE)
        return state[r, pl.ds(group, STRIPE), :]

    def self_energy(it, kind, real, imag, mirror_real, mirror_imag):
        real_square = real * real - imag * imag
        imag_square = 2.0 * real * imag
        coupling = weights[...]
        own = pl.ds(pl.multiple_of(tp * STRIPE, STRIPE), STRIPE)
        window[it, 2 * kind, own, :] = (
            coupling * (real_square * mirror_real - imag_square * mirror_imag)
        ).astype(BF16)
        window[it, 2 * kind + 1, own, :] = (
            coupling * (real_square * mirror_imag + imag_square * mirror_real)
        ).astype(BF16)

    def sigma_combined(state, it):
        later = iota((STRIPE, ROWS), 1) // NO < tp // 2
        real, imag = (
            jnp.where(later, column(state, r, 2), column(state, r, 0)) for r in range(2)
        )
        mirror_real, mirror_imag = (
            jnp.where(
                later,
                flip_in[it, 1, pl.ds(r * STRIPE, STRIPE), :].astype(F32),
                flip_own[pl.ds(r * STRIPE, STRIPE), :].astype(F32),
            )
            for r in range(2)
        )
        self_energy(it, 0, real, imag, mirror_real, mirror_imag)

    def sigma_middle(state, it):
        mirror_real, mirror_imag = (
            flip_in[it, 0, pl.ds(r * STRIPE, STRIPE), :].astype(F32) for r in range(2)
        )
        self_energy(
            it, 1, column(state, 0, 1), column(state, 1, 1), mirror_real, mirror_imag
        )

    def block(it, q):
        return window.at[it, :, pl.ds(pl.multiple_of(q * STRIPE, STRIPE), STRIPE), :]

    def send_block(it, q, target):
        remote(
            block(it, q), block(it, q), window_send.at[it], window_recv.at[it, q], (ta, target)
        ).start()

    def wait_block(it, q):
        wait_bytes(block(it, q), window_recv.at[it, q])

    near = zl + 1 - 2 * lax.rem(zl, 2)
    middle = 2 - zl // 2
    far = 3 * (1 - zl // 2)
    z_order = (zl, near, middle, far)

    def send_y(it, q):
        for dy in (1, 3, 2):
            send_block(it, q, lax.rem(tp + 8 * dy, N_TP))
        send_block(it, q, tp + 1 - 2 * core)

    def lefts(it, which, source, keep):
        for r in range(2):
            half = source[it, pl.ds(r * COLS, COLS), :]
            if keep is not None:
                half = jnp.where(keep, half, jnp.zeros_like(half))
            straight[which, pl.ds(r * COLS, COLS), :] = half
            crossed[which, pl.ds((1 - r) * COLS, COLS), :] = -half if r == 1 else half

    def multiply(it, dy):
        j = lax.rem(y + dy, N_Y)
        lanes = pl.ds(pl.multiple_of(j * 128, 128), 128)
        later = (j * 4 + iota((128, ROWS), 0) // NO) > iota((128, ROWS), 1) // NO
        old = jnp.where(later, 1.0, 0.0).astype(BF16)
        new = jnp.where(later, 0.0, 1.0).astype(BF16)
        left_parts, right_parts = [], []
        for r, side in ((0, straight), (1, crossed)):
            combined = window[it, r, lanes, :]
            right_parts += [combined * new, combined * old, window[it, 2 + r, lanes, :]]
            left_parts += [side[which, :, lanes] for which in range(3)]
        product = jnp.dot(
            jnp.concatenate(left_parts, axis=1),
            jnp.concatenate(right_parts, axis=0),
            preferred_element_type=F32,
        )
        if dy == 0:
            total[...] = product
        else:
            total[...] += product

    def hamilton_term(state):
        for r in range(2):
            for b in range(4):
                lanes = pl.ds(b * 128, 128)
                hamilton[pl.ds(r * COLS, COLS), lanes] = exact_dot(
                    state[r, :, lanes], blocked[...]
                )

    def prepare():
        squared = inter_ref[...] * inter_ref[...]
        pick = (iota((STRIPE, NO), 1) == core * STRIPE + iota((STRIPE, NO), 0)).astype(F32)
        picked = exact_dot(pick, squared, ((1,), (1,)))
        spread = (lax.rem(iota((NO, ROWS), 1), NO) == iota((NO, ROWS), 0)).astype(F32)
        weights[...] = exact_dot(picked, spread)
        tall = (lax.rem(iota((128, NO), 0), NO) == iota((128, NO), 1)).astype(F32)
        wide = (lax.rem(iota((NO, 128), 1), NO) == iota((NO, 128), 0)).astype(F32)
        across = exact_dot(exact_dot(tall, ham_ref[...], ((1,), (1,))), wide)
        same = iota((128, 128), 0) // NO == iota((128, 128), 1) // NO
        blocked[...] = jnp.where(same, across, 0.0)

    build_mirror(green_ref, 0)
    build_rounded(green_ref, 0)
    pl.semaphore_wait(barrier, N_TP - 1 + 2)

    for it in range(ITERS):
        state = green_ref if it == 0 else out_ref
        if it:
            build_mirror(state, it)
            build_rounded(state, it)
        send_mirror(it)
        rows = [row_copy(it, 2), row_copy(it, 1)]
        for copy in rows:
            copy.start()
        if it == 0:
            prepare()
        lefts(it, 0, rounded, None)
        wait_bytes(mirror_in.at[it, pl.ds(0, 31 * STRIPE), :], mirror_recv.at[it])
        flip(it)
        flips = [flip_copy(it, 1), flip_copy(it, 2)]
        for copy in flips:
            copy.start()
        hamilton_term(state)
        flips[1].wait_recv()
        sigma_combined(state, it)
        flips[0].wait_recv()
        sigma_middle(state, it)
        for z in (near, middle, far):
            send_block(it, tp, place(0, z, core))
        send_y(it, tp)
        for z in (near, middle, far):
            q = place(0, z, core)
            wait_block(it, q)
            send_y(it, q)
        rows[0].wait_recv()
        lefts(it, 2 - 1, earliest, ta >= 2)
        rows[1].wait_recv()
        lefts(it, 2, previous, ta >= 1)
        for z in z_order:
            wait_block(it, place(0, z, 1 - core))
        multiply(it, 0)
        for z in z_order:
            for dy in (1, 3, 2):
                q = place(dy, z, core)
                wait_block(it, q)
                send_block(it, q, tp + 1 - 2 * core)
        for dy in (1, 3, 2):
            for z in z_order:
                wait_block(it, place(dy, z, 1 - core))
            multiply(it, dy)
        out_real = state[0] + 0.5 * (
            hamilton[pl.ds(COLS, COLS), :] + FACTOR * total[pl.ds(COLS, COLS), :]
        )
        out_imag = state[1] - 0.5 * (
            hamilton[pl.ds(0, COLS), :] + FACTOR * total[pl.ds(0, COLS), :]
        )
        out_ref[0] = out_real
        out_ref[1] = out_imag
        wait_bytes(mirror_out.at[it, pl.ds(0, 31 * STRIPE), :], mirror_send.at[it])
        for copy in rows + flips:
            copy.wait_send()
        wait_bytes(window.at[it, :, pl.ds(0, 31 * STRIPE), :], window_send.at[it])


def shards(green, hamiltonian, interaction):
    shape = green.shape
    whole = pl.BlockSpec(memory_space=pltpu.VMEM)
    dma = pltpu.SemaphoreType.DMA
    result = pl.pallas_call(
        kernel,
        out_shape=jax.ShapeDtypeStruct((2, COLS, ROWS), F32),
        in_specs=[whole] * 3,
        out_specs=whole,
        scratch_shapes=[
            pltpu.VMEM((ITERS, 2 * COLS, ROWS), BF16),
            pltpu.VMEM((ITERS, 2 * COLS, ROWS), BF16),
            pltpu.VMEM((ITERS, 2 * COLS, ROWS), BF16),
            pltpu.VMEM((ITERS, ROWS, 128), BF16),
            pltpu.VMEM((ITERS, ROWS, 128), BF16),
            pltpu.VMEM((2 * STRIPE, ROWS), BF16),
            pltpu.VMEM((ITERS, 2, 2 * STRIPE, ROWS), BF16),
            pltpu.VMEM((ITERS, 2, 2 * STRIPE, ROWS), BF16),
            pltpu.VMEM((ITERS, 4, ROWS, ROWS), BF16),
            pltpu.VMEM((3, 2 * COLS, ROWS), BF16),
            pltpu.VMEM((3, 2 * COLS, ROWS), BF16),
            pltpu.VMEM((2 * COLS, ROWS), F32),
            pltpu.VMEM((2 * COLS, ROWS), F32),
            pltpu.VMEM((STRIPE, ROWS), F32),
            pltpu.VMEM((128, 128), F32),
            dma((ITERS, 2)),
            dma((ITERS, 2)),
            dma((ITERS,)),
            dma((ITERS,)),
            dma((ITERS, 2)),
            dma((ITERS, 2)),
            dma((ITERS,)),
            dma((ITERS, N_TP)),
        ],
        compiler_params=pltpu.CompilerParams(
            collective_id=0, has_side_effects=True, vmem_limit_bytes=48 * 2**20
        ),
        cost_estimate=pl.CostEstimate(
            flops=ITERS * 8 * COLS * 1536 * ROWS, bytes_accessed=4 * 2**20, transcendentals=0
        ),
    )(green.reshape(2, COLS, ROWS), hamiltonian, interaction)
    return result.reshape(shape)


def solution(mesh):
    in_specs = (P(None, None, "tp", None, "ta"), P(), P())
    out_specs = P(None, None, "tp", None, "ta")
    return jax.shard_map(shards, mesh=mesh, in_specs=in_specs, out_specs=out_specs, check_vma=False)
```

```python
import functools

import jax
import jax.numpy as jnp
from jax import lax
from jax.experimental import pallas as pl
from jax.experimental.pallas import tpu as pltpu
from jax.sharding import PartitionSpec as P

NO = 32
ITERS = 2
N_TA = 8
N_TP = 32
N_Y = 4
N_Z = 4
STRIPE = 16
ROWS = 512
COLS = 128
FACTOR = 1.0 / 32.0
PIECES = ((0, 2, 0, 256), (0, 1, 0, 64), (2, 1, 64, 64), (5, 1, 128, 128))

MESH = pl.DeviceIdType.MESH
HIGHEST = lax.Precision.HIGHEST
F32 = jnp.float32
BF16 = jnp.bfloat16


def iota(shape, dim):
    return lax.broadcasted_iota(jnp.int32, shape, dim)


def exact_dot(left, right, contract=((1,), (0,))):
    return lax.dot_general(
        left, right, (contract, ((), ())), precision=HIGHEST, preferred_element_type=F32
    )


def kernel(
    green_hbm,
    ham_hbm,
    inter_hbm,
    out_ref,
    green_ref,
    ham_ref,
    inter_ref,
    rounded,
    previous,
    earliest,
    mirror_out,
    mirror_in,
    flip_own,
    flip_out,
    flip_in,
    window,
    straight,
    crossed,
    total,
    hamilton,
    weights,
    blocked,
    row_send,
    row_recv,
    mirror_send,
    mirror_recv,
    flip_send,
    flip_recv,
    window_send,
    window_recv,
    input_sem,
):
    ta = lax.axis_index("ta")
    tp = lax.axis_index("tp")
    y = tp // 8
    zl = lax.rem(tp // 2, 4)
    core = lax.rem(tp, 2)

    def ta_plus(k):
        return lax.rem(ta + k + N_TA, N_TA)

    near = zl + 1 - 2 * lax.rem(zl, 2)
    middle = 2 - zl // 2
    far = 3 * (1 - zl // 2)

    def stripe_of(q):
        return pl.ds(pl.multiple_of(q * STRIPE, STRIPE), STRIPE)

    def place(dy, z, c):
        return lax.rem(y + dy, N_Y) * 8 + z * 2 + c

    inputs = [
        pltpu.make_async_copy(src, dst, input_sem.at[n])
        for n, (src, dst) in enumerate(
            ((green_hbm, green_ref), (ham_hbm, ham_ref), (inter_hbm, inter_ref))
        )
    ]
    for copy in inputs:
        copy.start()

    barrier = pltpu.get_barrier_semaphore()

    def greet(k, carry):
        pl.semaphore_signal(
            barrier, inc=1, device_id=(ta, lax.rem(tp + k, N_TP)), device_id_type=MESH
        )
        return carry

    lax.fori_loop(1, N_TP, greet, 0)
    for k in (1, 2):
        pl.semaphore_signal(
            barrier, inc=1, device_id=(ta_plus(-k), tp), device_id_type=MESH
        )

    def remote(src, dst, send, recv, target):
        return pltpu.make_async_remote_copy(
            src_ref=src,
            dst_ref=dst,
            send_sem=send,
            recv_sem=recv,
            device_id=target,
            device_id_type=MESH,
        )

    def build_mirror(state, it):
        pieces = []
        for k in range(3):
            group = pl.multiple_of(ta_plus(k) * STRIPE, STRIPE)
            for r in range(2):
                pieces.append(state[r, pl.ds(group, STRIPE), :])
        pieces.append(jnp.zeros((2 * STRIPE, ROWS), F32))
        stacked = jnp.concatenate(pieces, axis=0)
        mirror_out[it] = stacked.T.astype(BF16)

    def build_rounded(state, it):
        for r in range(2):
            rounded[it, pl.ds(r * COLS, COLS), :] = state[r].astype(BF16)

    def row_copy(it, n):
        k, start, count = PIECES[n][1:]
        return remote(
            rounded.at[it, pl.ds(start, count)],
            (previous if k == 1 else earliest).at[it, pl.ds(start, count)],
            row_send.at[it, n],
            row_recv.at[it, n],
            (ta_plus(k), tp),
        )

    def flip_copy(it, k):
        return remote(
            flip_out.at[it, k - 1],
            flip_in.at[it, k - 1],
            flip_send.at[it, k - 1],
            flip_recv.at[it, k - 1],
            (ta_plus(k), tp),
        )

    def send_mirror(it):
        for dy in (2, 1, 3, 0):
            for z in (far, middle, near, zl):
                for flip_core in (1, 0):
                    if dy == 0 and z is zl and flip_core == 0:
                        continue
                    c = 1 - core if flip_core else core
                    peer = place(dy, z, c)
                    remote(
                        mirror_out.at[it, stripe_of(peer), :],
                        mirror_in.at[it, stripe_of(tp), :],
                        mirror_send.at[it],
                        mirror_recv.at[it],
                        (ta, peer),
                    ).start()
        mirror_in[it, stripe_of(tp), :] = mirror_out[it, stripe_of(tp), :]

    def wait_bytes(ref, sem):
        pltpu.make_async_copy(ref, ref, sem).wait()

    def flip(it):
        piece = iota((STRIPE, 128), 1) // STRIPE
        for j in range(4):
            parts = [
                mirror_in[it, pl.ds((j * 8 + i) * STRIPE, STRIPE), :].astype(F32)
                for i in range(8)
            ]
            for bit in (1, 2, 4):
                low = (piece // bit) % 2 == 0
                for i in range(8):
                    if i & bit:
                        continue
                    first, second = parts[i], parts[i | bit]
                    parts[i] = jnp.where(low, first, pltpu.roll(second, STRIPE * bit, 1))
                    parts[i | bit] = jnp.where(
                        low, pltpu.roll(first, 128 - STRIPE * bit, 1), second
                    )
            for k in range(3):
                both = jnp.concatenate([parts[2 * k], parts[2 * k + 1]], axis=0).astype(BF16)
                lanes = pl.ds(j * 128, 128)
                if k == 0:
                    flip_own[:, lanes] = both
                else:
                    flip_out[it, k - 1, :, lanes] = both

    def column(state, r, k):
        group = pl.multiple_of(ta_plus(-k) * STRIPE, STRIPE)
        return state[r, pl.ds(group, STRIPE), :]

    def self_energy(it, kind, real, imag, mirror_real, mirror_imag):
        real_square = real * real - imag * imag
        imag_square = 2.0 * real * imag
        coupling = weights[...]
        window[it, 2 * kind, y, zl, core] = (
            coupling * (real_square * mirror_real - imag_square * mirror_imag)
        ).astype(BF16)
        window[it, 2 * kind + 1, y, zl, core] = (
            coupling * (real_square * mirror_imag + imag_square * mirror_real)
        ).astype(BF16)

    def sigma_combined(state, it):
        later = iota((STRIPE, ROWS), 1) // NO < tp // 2
        real, imag = (
            jnp.where(later, column(state, r, 2), column(state, r, 0)) for r in range(2)
        )
        mirror_real, mirror_imag = (
            jnp.where(
                later,
                flip_in[it, 1, pl.ds(r * STRIPE, STRIPE), :].astype(F32),
                flip_own[pl.ds(r * STRIPE, STRIPE), :].astype(F32),
            )
            for r in range(2)
        )
        self_energy(it, 0, real, imag, mirror_real, mirror_imag)

    def sigma_middle(state, it):
        mirror_real, mirror_imag = (
            flip_in[it, 0, pl.ds(r * STRIPE, STRIPE), :].astype(F32) for r in range(2)
        )
        self_energy(
            it, 1, column(state, 0, 1), column(state, 1, 1), mirror_real, mirror_imag
        )

    def send_own(it, kind):
        part = window.at[it, pl.ds(2 * kind, 2), y, :, core]
        for z in (near, middle, far):
            remote(
                part.at[:, zl],
                part.at[:, zl],
                window_send.at[it],
                window_recv.at[it, kind, zl],
                (ta, place(0, z, core)),
            ).start()

    def wait_z(it, kind, z):
        part = window.at[it, pl.ds(2 * kind, 2), y, :, core]
        wait_bytes(part.at[:, z], window_recv.at[it, kind, z])

    def pair_part(it, kind, dy, pair):
        return window.at[
            it, pl.ds(2 * kind, 2), lax.rem(y + dy, N_Y), pl.ds(2 * pair, 2), core
        ]

    def send_pair(it, kind, pair):
        part = pair_part(it, kind, 0, pair)
        for dy in (2, 1, 3):
            remote(
                part,
                part,
                window_send.at[it],
                window_recv.at[it, kind, 4 + 4 * pair + y],
                (ta, place(dy, zl, core)),
            ).start()

    def wait_pair(it, kind, dy, pair):
        wait_bytes(
            pair_part(it, kind, dy, pair),
            window_recv.at[it, kind, 4 + 4 * pair + lax.rem(y + dy, N_Y)],
        )

    def send_sibling(it, kind, dy):
        j = lax.rem(y + dy, N_Y)
        part = window.at[it, pl.ds(2 * kind, 2), j, :, core]
        remote(
            part,
            part,
            window_send.at[it],
            window_recv.at[it, kind, 12 + j],
            (ta, place(0, zl, 1 - core)),
        ).start()

    def wait_sibling(it, kind, dy):
        j = lax.rem(y + dy, N_Y)
        wait_bytes(
            window.at[it, pl.ds(2 * kind, 2), j, :, 1 - core], window_recv.at[it, kind, 12 + j]
        )

    def lefts(it, which, source, keep):
        for r in range(2):
            half = source[it, pl.ds(r * COLS, COLS), :]
            if keep is not None:
                half = jnp.where(keep, half, jnp.zeros_like(half))
            straight[which, pl.ds(r * COLS, COLS), :] = half
            crossed[which, pl.ds((1 - r) * COLS, COLS), :] = -half if r == 1 else half

    def rows_of(it, part, j):
        return window[it, part, j].reshape(128, ROWS)

    def multiply_combined(it, dy):
        j = lax.rem(y + dy, N_Y)
        lanes = pl.ds(pl.multiple_of(j * 128, 128), 128)
        later = (j * 4 + iota((128, ROWS), 0) // NO) > iota((128, ROWS), 1) // NO
        old = jnp.where(later, 1.0, 0.0).astype(BF16)
        new = jnp.where(later, 0.0, 1.0).astype(BF16)
        left_parts, right_parts = [], []
        for r, side in ((0, straight), (1, crossed)):
            combined = rows_of(it, r, j)
            right_parts += [combined * new, combined * old]
            left_parts += [side[which, :, lanes] for which in range(2)]
        product = jnp.dot(
            jnp.concatenate(left_parts, axis=1),
            jnp.concatenate(right_parts, axis=0),
            preferred_element_type=F32,
        )
        if dy == 0:
            total[...] = product
        else:
            total[...] += product

    def multiply_middle(it):
        total[...] += sum(
            jnp.dot(
                side[2], window[it, 2 + r].reshape(ROWS, ROWS), preferred_element_type=F32
            )
            for r, side in ((0, straight), (1, crossed))
        )

    def hamilton_term(state):
        for r in range(2):
            for b in range(4):
                lanes = pl.ds(b * 128, 128)
                hamilton[pl.ds(r * COLS, COLS), lanes] = exact_dot(
                    state[r, :, lanes], blocked[...]
                )

    def prepare():
        squared = inter_ref[...] * inter_ref[...]
        pick = (iota((STRIPE, NO), 1) == core * STRIPE + iota((STRIPE, NO), 0)).astype(F32)
        picked = exact_dot(pick, squared, ((1,), (1,)))
        spread = (lax.rem(iota((NO, ROWS), 1), NO) == iota((NO, ROWS), 0)).astype(F32)
        weights[...] = exact_dot(picked, spread)
        tall = (lax.rem(iota((128, NO), 0), NO) == iota((128, NO), 1)).astype(F32)
        wide = (lax.rem(iota((NO, 128), 1), NO) == iota((NO, 128), 0)).astype(F32)
        across = exact_dot(exact_dot(tall, ham_ref[...], ((1,), (1,))), wide)
        same = iota((128, 128), 0) // NO == iota((128, 128), 1) // NO
        blocked[...] = jnp.where(same, across, 0.0)

    for copy in inputs:
        copy.wait()
    build_mirror(green_ref, 0)
    build_rounded(green_ref, 0)
    pl.semaphore_wait(barrier, N_TP - 1 + 2)

    for it in range(ITERS):
        state = green_ref if it == 0 else out_ref
        if it:
            build_mirror(state, it)
            build_rounded(state, it)
        rows = [row_copy(it, n) for n in range(len(PIECES))]

        def start_rows(stage):
            for piece, copy in zip(PIECES, rows):
                if piece[0] == stage:
                    copy.start()

        def wait_rows(k):
            for piece, copy in zip(PIECES, rows):
                if piece[1] == k:
                    copy.wait_recv()

        send_mirror(it)
        start_rows(0)
        if it == 0:
            prepare()
        lefts(it, 0, rounded, None)
        wait_bytes(mirror_in.at[it, pl.ds(0, 31 * STRIPE), :], mirror_recv.at[it])
        start_rows(1)
        flip(it)
        flips = [flip_copy(it, 1), flip_copy(it, 2)]
        for copy in flips:
            copy.start()
        start_rows(2)
        hamilton_term(state)
        flips[1].wait_recv()
        sigma_combined(state, it)
        send_own(it, 0)
        start_rows(3)
        flips[0].wait_recv()
        sigma_middle(state, it)
        send_own(it, 1)
        start_rows(4)
        own_pair = zl // 2
        wait_rows(2)
        lefts(it, 1, earliest, ta >= 2)
        for kind in range(2):
            wait_z(it, kind, near)
            send_pair(it, kind, own_pair)
        for kind in range(2):
            wait_z(it, kind, middle)
            wait_z(it, kind, far)
            send_pair(it, kind, 1 - own_pair)
            send_sibling(it, kind, 0)
        start_rows(5)
        wait_sibling(it, 0, 0)
        multiply_combined(it, 0)
        for kind in range(2):
            for dy in (1, 3, 2):
                wait_pair(it, kind, dy, own_pair)
                wait_pair(it, kind, dy, 1 - own_pair)
                send_sibling(it, kind, dy)
        for dy in (1, 3, 2):
            wait_sibling(it, 0, dy)
            multiply_combined(it, dy)
        wait_rows(1)
        lefts(it, 2, previous, ta >= 1)
        for dy in range(4):
            wait_sibling(it, 1, dy)
        multiply_middle(it)
        out_real = state[0] + 0.5 * (
            hamilton[pl.ds(COLS, COLS), :] + FACTOR * total[pl.ds(COLS, COLS), :]
        )
        out_imag = state[1] - 0.5 * (
            hamilton[pl.ds(0, COLS), :] + FACTOR * total[pl.ds(0, COLS), :]
        )
        out_ref[0] = out_real
        out_ref[1] = out_imag
        wait_bytes(mirror_out.at[it, pl.ds(0, 31 * STRIPE), :], mirror_send.at[it])
        for copy in rows + flips:
            copy.wait_send()
        wait_bytes(window.at[it, :, pl.ds(0, 3)], window_send.at[it])
        wait_bytes(window.at[it, :, 3, pl.ds(0, 3)], window_send.at[it])
        wait_bytes(window.at[it, :, 3, 3, 0], window_send.at[it])


def shards(green, hamiltonian, interaction):
    shape = green.shape
    whole = pl.BlockSpec(memory_space=pltpu.VMEM)
    dma = pltpu.SemaphoreType.DMA
    result = pl.pallas_call(
        kernel,
        out_shape=jax.ShapeDtypeStruct((2, COLS, ROWS), F32),
        in_specs=[pl.BlockSpec(memory_space=pltpu.HBM)] * 3,
        out_specs=whole,
        scratch_shapes=[
            pltpu.VMEM((2, COLS, ROWS), F32),
            pltpu.VMEM((NO, NO), F32),
            pltpu.VMEM((NO, NO), F32),
            pltpu.VMEM((ITERS, 2 * COLS, ROWS), BF16),
            pltpu.VMEM((ITERS, 2 * COLS, ROWS), BF16),
            pltpu.VMEM((ITERS, 2 * COLS, ROWS), BF16),
            pltpu.VMEM((ITERS, ROWS, 128), BF16),
            pltpu.VMEM((ITERS, ROWS, 128), BF16),
            pltpu.VMEM((2 * STRIPE, ROWS), BF16),
            pltpu.VMEM((ITERS, 2, 2 * STRIPE, ROWS), BF16),
            pltpu.VMEM((ITERS, 2, 2 * STRIPE, ROWS), BF16),
            pltpu.VMEM((ITERS, 4, N_Y, N_Z, 2, STRIPE, ROWS), BF16),
            pltpu.VMEM((3, 2 * COLS, ROWS), BF16),
            pltpu.VMEM((3, 2 * COLS, ROWS), BF16),
            pltpu.VMEM((2 * COLS, ROWS), F32),
            pltpu.VMEM((2 * COLS, ROWS), F32),
            pltpu.VMEM((STRIPE, ROWS), F32),
            pltpu.VMEM((128, 128), F32),
            dma((ITERS, len(PIECES))),
            dma((ITERS, len(PIECES))),
            dma((ITERS,)),
            dma((ITERS,)),
            dma((ITERS, 2)),
            dma((ITERS, 2)),
            dma((ITERS,)),
            dma((ITERS, 2, 16)),
            dma((3,)),
        ],
        compiler_params=pltpu.CompilerParams(
            collective_id=0, has_side_effects=True, vmem_limit_bytes=48 * 2**20
        ),
        cost_estimate=pl.CostEstimate(
            flops=ITERS * 8 * COLS * 1536 * ROWS, bytes_accessed=4 * 2**20, transcendentals=0
        ),
    )(green.reshape(2, COLS, ROWS), hamiltonian, interaction)
    return result.reshape(shape)


def solution(mesh):
    in_specs = (P(None, None, "tp", None, "ta"), P(), P())
    out_specs = P(None, None, "tp", None, "ta")
    return jax.shard_map(shards, mesh=mesh, in_specs=in_specs, out_specs=out_specs, check_vma=False)
```

```python
import functools

import jax
import jax.numpy as jnp
from jax import lax
from jax.experimental import pallas as pl
from jax.experimental.pallas import tpu as pltpu
from jax.sharding import PartitionSpec as P

NO = 32
ITERS = 2
N_TA = 8
N_TP = 32
N_Y = 4
N_Z = 4
STRIPE = 16
ROWS = 512
COLS = 128
FACTOR = 1.0 / 32.0
PIECES = ((4, 2, 0, 256), (0, 1, 0, 128), (5, 1, 128, 128))

MESH = pl.DeviceIdType.MESH
HIGHEST = lax.Precision.HIGHEST
F32 = jnp.float32
BF16 = jnp.bfloat16


def iota(shape, dim):
    return lax.broadcasted_iota(jnp.int32, shape, dim)


def exact_dot(left, right, contract=((1,), (0,))):
    return lax.dot_general(
        left, right, (contract, ((), ())), precision=HIGHEST, preferred_element_type=F32
    )


def kernel(
    green_hbm,
    ham_hbm,
    inter_hbm,
    out_ref,
    green_ref,
    ham_ref,
    inter_ref,
    rounded,
    previous,
    earliest,
    stage_out,
    stage_in,
    mirror_out,
    mirror_in,
    flipped,
    window,
    straight,
    crossed,
    total,
    hamilton,
    weights,
    blocked,
    row_send,
    row_recv,
    stage_send,
    stage_recv,
    mirror_send,
    mirror_recv,
    window_send,
    window_recv,
    input_sem,
):
    ta = lax.axis_index("ta")
    tp = lax.axis_index("tp")
    y = tp // 8
    zl = lax.rem(tp // 2, 4)
    core = lax.rem(tp, 2)

    def ta_plus(k):
        return lax.rem(ta + k + N_TA, N_TA)

    near = zl + 1 - 2 * lax.rem(zl, 2)
    middle = 2 - zl // 2
    far = 3 * (1 - zl // 2)
    z_order = (zl, near, middle, far)

    def stripe_of(q):
        return pl.ds(pl.multiple_of(q * STRIPE, STRIPE), STRIPE)

    def place(dy, z, c):
        return lax.rem(y + dy, N_Y) * 8 + z * 2 + c

    inputs = [
        pltpu.make_async_copy(src, dst, input_sem.at[n])
        for n, (src, dst) in enumerate(
            ((green_hbm, green_ref), (ham_hbm, ham_ref), (inter_hbm, inter_ref))
        )
    ]
    for copy in inputs:
        copy.start()

    barrier = pltpu.get_barrier_semaphore()

    for dy in (1, 2, 3):
        pl.semaphore_signal(
            barrier, inc=1, device_id=(ta, place(dy, zl, core)), device_id_type=MESH
        )
    for k in (1, 2, 0):
        for z in (far, middle, near, zl):
            for other in (1, 0):
                if k == 0 and z is zl and other == 0:
                    continue
                c = 1 - core if other else core
                pl.semaphore_signal(
                    barrier,
                    inc=1,
                    device_id=(ta_plus(-k), place(0, z, c)),
                    device_id_type=MESH,
                )

    def remote(src, dst, send, recv, target):
        return pltpu.make_async_remote_copy(
            src_ref=src,
            dst_ref=dst,
            send_sem=send,
            recv_sem=recv,
            device_id=target,
            device_id_type=MESH,
        )

    def build_stage(state, it):
        for k in range(3):
            group = pl.multiple_of(ta_plus(k) * STRIPE, STRIPE)
            for r in range(2):
                piece = state[r, pl.ds(group, STRIPE), :].astype(BF16)
                for j in range(N_Y):
                    stage_out[it, j, pl.ds((2 * k + r) * STRIPE, STRIPE), :] = piece[
                        :, j * 128 : (j + 1) * 128
                    ]

    def build_rounded(state, it):
        for r in range(2):
            rounded[it, pl.ds(r * COLS, COLS), :] = state[r].astype(BF16)

    def row_copy(it, n):
        k, start, count = PIECES[n][1:]
        return remote(
            rounded.at[it, pl.ds(start, count)],
            (previous if k == 1 else earliest).at[it, pl.ds(start, count)],
            row_send.at[it, n],
            row_recv.at[it, n],
            (ta_plus(k), tp),
        )

    def stage_copy(it, dy):
        j = lax.rem(y + dy, N_Y)
        return remote(
            stage_out.at[it, j],
            stage_in.at[it, y],
            stage_send.at[it, dy - 1],
            stage_recv.at[it, dy - 1],
            (ta, place(dy, zl, core)),
        )

    def build_mirror(it):
        stage_in[it, y] = stage_out[it, y]
        for k in (1, 2, 0):
            stacked = jnp.concatenate(
                [stage_in[it, j, pl.ds(2 * k * STRIPE, 2 * STRIPE), :] for j in range(N_Y)],
                axis=0,
            )
            mirror_out[it, k] = stacked.astype(F32).T.astype(BF16)
            send_mirror(it, k)
        own = stripe_of(zl * 2 + core)
        mirror_in[it, 0, own, :] = mirror_out[it, 0, own, :]

    def send_mirror(it, k):
        for z in (far, middle, near, zl):
            for other in (1, 0):
                if k == 0 and z is zl and other == 0:
                    continue
                c = 1 - core if other else core
                remote(
                    mirror_out.at[it, k, stripe_of(z * 2 + c), :],
                    mirror_in.at[it, k, stripe_of(zl * 2 + core), :],
                    mirror_send.at[it, k],
                    mirror_recv.at[it, k],
                    (ta_plus(k), place(0, z, c)),
                ).start()

    def mirror_bytes(ref, it, k):
        return ref.at[it, k] if k else ref.at[it, 0, pl.ds(0, 7 * STRIPE), :]

    def wait_bytes(ref, sem):
        pltpu.make_async_copy(ref, ref, sem).wait()

    def flip(it, k):
        piece = iota((STRIPE, 128), 1) // STRIPE
        parts = [
            mirror_in[it, k, pl.ds(i * STRIPE, STRIPE), :].astype(F32) for i in range(8)
        ]
        for bit in (1, 2, 4):
            low = (piece // bit) % 2 == 0
            for i in range(8):
                if i & bit:
                    continue
                first, second = parts[i], parts[i | bit]
                parts[i] = jnp.where(low, first, pltpu.roll(second, STRIPE * bit, 1))
                parts[i | bit] = jnp.where(
                    low, pltpu.roll(first, 128 - STRIPE * bit, 1), second
                )
        for j in range(N_Y):
            for r in range(2):
                flipped[k, r, :, pl.ds(j * 128, 128)] = parts[2 * j + r]

    def column(state, r, k):
        group = pl.multiple_of(ta_plus(-k) * STRIPE, STRIPE)
        return state[r, pl.ds(group, STRIPE), :]

    def self_energy(it, kind, real, imag, mirror_real, mirror_imag):
        real_square = real * real - imag * imag
        imag_square = 2.0 * real * imag
        coupling = weights[...]
        window[it, 2 * kind, y, zl, core] = (
            coupling * (real_square * mirror_real - imag_square * mirror_imag)
        ).astype(BF16)
        window[it, 2 * kind + 1, y, zl, core] = (
            coupling * (real_square * mirror_imag + imag_square * mirror_real)
        ).astype(BF16)

    def sigma_combined(state, it):
        later = iota((STRIPE, ROWS), 1) // NO < tp // 2
        real, imag = (
            jnp.where(later, column(state, r, 2), column(state, r, 0)) for r in range(2)
        )
        mirror_real, mirror_imag = (
            jnp.where(later, flipped[2, r], flipped[0, r]) for r in range(2)
        )
        self_energy(it, 0, real, imag, mirror_real, mirror_imag)

    def sigma_middle(state, it):
        self_energy(
            it, 1, column(state, 0, 1), column(state, 1, 1), flipped[1, 0], flipped[1, 1]
        )

    def send_own(it, kind):
        part = window.at[it, pl.ds(2 * kind, 2), y, :, core]
        for z in (near, middle, far):
            remote(
                part.at[:, zl],
                part.at[:, zl],
                window_send.at[it],
                window_recv.at[it, kind, zl],
                (ta, place(0, z, core)),
            ).start()

    def wait_z(it, kind, z):
        part = window.at[it, pl.ds(2 * kind, 2), y, :, core]
        wait_bytes(part.at[:, z], window_recv.at[it, kind, z])

    def y_part(it, kind, dy, piece):
        part = window.at[it, pl.ds(2 * kind, 2), lax.rem(y + dy, N_Y)]
        return part.at[:, z_order[piece], core]

    def y_copy(it, kind, piece, source, target):
        part = y_part(it, kind, source, piece)
        return remote(
            part,
            part,
            window_send.at[it],
            window_recv.at[it, kind, 4 + 4 * piece + lax.rem(y + source, N_Y)],
            (ta, place(target, zl, core)),
        )

    def send_y(it, kind, piece):
        for dy in (2, 1, 3) if piece == 3 else (1, 3):
            y_copy(it, kind, piece, 0, dy).start()

    def wait_y(it, kind, piece, dy):
        wait_bytes(
            y_part(it, kind, dy, piece),
            window_recv.at[it, kind, 4 + 4 * piece + lax.rem(y + dy, N_Y)],
        )

    def relay(it, kind, piece):
        source, target = ((3, 1), (1, 3))[kind]
        wait_y(it, kind, piece, source)
        y_copy(it, kind, piece, source, target).start()

    def send_sibling(it, kind, dy):
        j = lax.rem(y + dy, N_Y)
        part = window.at[it, pl.ds(2 * kind, 2), j, :, core]
        remote(
            part,
            part,
            window_send.at[it],
            window_recv.at[it, kind, 20 + j],
            (ta, place(0, zl, 1 - core)),
        ).start()

    def wait_sibling(it, kind, dy):
        j = lax.rem(y + dy, N_Y)
        wait_bytes(
            window.at[it, pl.ds(2 * kind, 2), j, :, 1 - core], window_recv.at[it, kind, 20 + j]
        )

    def lefts(it, which, source, keep):
        for r in range(2):
            half = source[it, pl.ds(r * COLS, COLS), :]
            if keep is not None:
                half = jnp.where(keep, half, jnp.zeros_like(half))
            straight[which, pl.ds(r * COLS, COLS), :] = half
            crossed[which, pl.ds((1 - r) * COLS, COLS), :] = -half if r == 1 else half

    def rows_of(it, part, j):
        return window[it, part, j].reshape(128, ROWS)

    def multiply_combined(it, dy):
        j = lax.rem(y + dy, N_Y)
        lanes = pl.ds(pl.multiple_of(j * 128, 128), 128)
        later = (j * 4 + iota((128, ROWS), 0) // NO) > iota((128, ROWS), 1) // NO
        old = jnp.where(later, 1.0, 0.0).astype(BF16)
        new = jnp.where(later, 0.0, 1.0).astype(BF16)
        left_parts, right_parts = [], []
        for r, side in ((0, straight), (1, crossed)):
            combined = rows_of(it, r, j)
            right_parts += [combined * new, combined * old]
            left_parts += [side[which, :, lanes] for which in range(2)]
        product = jnp.dot(
            jnp.concatenate(left_parts, axis=1),
            jnp.concatenate(right_parts, axis=0),
            preferred_element_type=F32,
        )
        if dy == 0:
            total[...] = product
        else:
            total[...] += product

    def multiply_middle(it, dy):
        j = lax.rem(y + dy, N_Y)
        lanes = pl.ds(pl.multiple_of(j * 128, 128), 128)
        total[...] += jnp.dot(
            jnp.concatenate([straight[2, :, lanes], crossed[2, :, lanes]], axis=1),
            jnp.concatenate([rows_of(it, 2, j), rows_of(it, 3, j)], axis=0),
            preferred_element_type=F32,
        )

    def hamilton_term(state):
        for r in range(2):
            for b in range(4):
                lanes = pl.ds(b * 128, 128)
                hamilton[pl.ds(r * COLS, COLS), lanes] = exact_dot(
                    state[r, :, lanes], blocked[...]
                )

    def prepare():
        squared = inter_ref[...] * inter_ref[...]
        pick = (iota((STRIPE, NO), 1) == core * STRIPE + iota((STRIPE, NO), 0)).astype(F32)
        picked = exact_dot(pick, squared, ((1,), (1,)))
        spread = (lax.rem(iota((NO, ROWS), 1), NO) == iota((NO, ROWS), 0)).astype(F32)
        weights[...] = exact_dot(picked, spread)
        tall = (lax.rem(iota((128, NO), 0), NO) == iota((128, NO), 1)).astype(F32)
        wide = (lax.rem(iota((NO, 128), 1), NO) == iota((NO, 128), 0)).astype(F32)
        across = exact_dot(exact_dot(tall, ham_ref[...], ((1,), (1,))), wide)
        same = iota((128, 128), 0) // NO == iota((128, 128), 1) // NO
        blocked[...] = jnp.where(same, across, 0.0)

    for copy in inputs:
        copy.wait()
    build_stage(green_ref, 0)
    pl.semaphore_wait(barrier, 26)

    for it in range(ITERS):
        state = green_ref if it == 0 else out_ref
        if it:
            build_stage(state, it)
        stages = [stage_copy(it, dy) for dy in (1, 2, 3)]
        for n in (1, 0, 2):
            stages[n].start()
        build_rounded(state, it)
        rows = [row_copy(it, n) for n in range(len(PIECES))]

        def start_rows(stage):
            for piece, copy in zip(PIECES, rows):
                if piece[0] == stage:
                    copy.start()

        def wait_rows(k):
            for piece, copy in zip(PIECES, rows):
                if piece[1] == k:
                    copy.wait_recv()

        start_rows(0)
        if it == 0:
            prepare()
        lefts(it, 0, rounded, None)
        for copy in stages:
            copy.wait_recv()
        build_mirror(it)
        start_rows(1)
        hamilton_term(state)
        for k in (0, 2):
            wait_bytes(mirror_bytes(mirror_in, it, k), mirror_recv.at[it, k])
            flip(it, k)
        sigma_combined(state, it)
        send_own(it, 0)
        send_y(it, 0, 0)
        start_rows(3)
        wait_bytes(mirror_bytes(mirror_in, it, 1), mirror_recv.at[it, 1])
        flip(it, 1)
        sigma_middle(state, it)
        send_own(it, 1)
        send_y(it, 1, 0)
        start_rows(4)
        for kind in range(2):
            wait_z(it, kind, near)
            send_y(it, kind, 1)
        for kind in range(2):
            relay(it, kind, 0)
        for kind in range(2):
            wait_z(it, kind, middle)
            send_y(it, kind, 2)
        for kind in range(2):
            relay(it, kind, 1)
        for kind in range(2):
            wait_z(it, kind, far)
            send_y(it, kind, 3)
            send_sibling(it, kind, 0)
        start_rows(5)
        for kind in range(2):
            relay(it, kind, 2)
        for kind in range(2):
            dy = 3 if kind == 0 else 1
            wait_y(it, kind, 3, dy)
            send_sibling(it, kind, dy)
        for kind in range(2):
            dy = 1 if kind == 0 else 3
            for piece in range(4):
                wait_y(it, kind, piece, dy)
            send_sibling(it, kind, dy)
        wait_rows(2)
        lefts(it, 1, earliest, ta >= 2)
        wait_sibling(it, 0, 0)
        multiply_combined(it, 0)
        for piece in range(4):
            wait_y(it, 0, piece, 2)
        send_sibling(it, 0, 2)
        for dy in (3, 1):
            wait_sibling(it, 0, dy)
            multiply_combined(it, dy)
        for piece in range(4):
            wait_y(it, 1, piece, 2)
        send_sibling(it, 1, 2)
        wait_rows(1)
        lefts(it, 2, previous, ta >= 1)
        for dy in (0, 1, 3):
            wait_sibling(it, 1, dy)
            multiply_middle(it, dy)
        wait_sibling(it, 0, 2)
        multiply_combined(it, 2)
        wait_sibling(it, 1, 2)
        multiply_middle(it, 2)
        out_real = state[0] + 0.5 * (
            hamilton[pl.ds(COLS, COLS), :] + FACTOR * total[pl.ds(COLS, COLS), :]
        )
        out_imag = state[1] - 0.5 * (
            hamilton[pl.ds(0, COLS), :] + FACTOR * total[pl.ds(0, COLS), :]
        )
        out_ref[0] = out_real
        out_ref[1] = out_imag
        for k in range(3):
            wait_bytes(mirror_bytes(mirror_out, it, k), mirror_send.at[it, k])
        for copy in rows + stages:
            copy.wait_send()
        wait_bytes(window.at[it, :, pl.ds(0, 3)], window_send.at[it])
        wait_bytes(window.at[it, :, 3, pl.ds(0, 3)], window_send.at[it])
        wait_bytes(window.at[it, :, 3, 3, 0], window_send.at[it])


def shards(green, hamiltonian, interaction):
    shape = green.shape
    whole = pl.BlockSpec(memory_space=pltpu.VMEM)
    dma = pltpu.SemaphoreType.DMA
    result = pl.pallas_call(
        kernel,
        out_shape=jax.ShapeDtypeStruct((2, COLS, ROWS), F32),
        in_specs=[pl.BlockSpec(memory_space=pltpu.HBM)] * 3,
        out_specs=whole,
        scratch_shapes=[
            pltpu.VMEM((2, COLS, ROWS), F32),
            pltpu.VMEM((NO, NO), F32),
            pltpu.VMEM((NO, NO), F32),
            pltpu.VMEM((ITERS, 2 * COLS, ROWS), BF16),
            pltpu.VMEM((ITERS, 2 * COLS, ROWS), BF16),
            pltpu.VMEM((ITERS, 2 * COLS, ROWS), BF16),
            pltpu.VMEM((ITERS, N_Y, 6 * STRIPE, 128), BF16),
            pltpu.VMEM((ITERS, N_Y, 6 * STRIPE, 128), BF16),
            pltpu.VMEM((ITERS, 3, 128, 128), BF16),
            pltpu.VMEM((ITERS, 3, 128, 128), BF16),
            pltpu.VMEM((3, 2, STRIPE, ROWS), F32),
            pltpu.VMEM((ITERS, 4, N_Y, N_Z, 2, STRIPE, ROWS), BF16),
            pltpu.VMEM((3, 2 * COLS, ROWS), BF16),
            pltpu.VMEM((3, 2 * COLS, ROWS), BF16),
            pltpu.VMEM((2 * COLS, ROWS), F32),
            pltpu.VMEM((2 * COLS, ROWS), F32),
            pltpu.VMEM((STRIPE, ROWS), F32),
            pltpu.VMEM((128, 128), F32),
            dma((ITERS, len(PIECES))),
            dma((ITERS, len(PIECES))),
            dma((ITERS, 3)),
            dma((ITERS, 3)),
            dma((ITERS, 3)),
            dma((ITERS, 3)),
            dma((ITERS,)),
            dma((ITERS, 2, 24)),
            dma((3,)),
        ],
        compiler_params=pltpu.CompilerParams(
            collective_id=0, has_side_effects=True, vmem_limit_bytes=63 * 2**20 + 900000
        ),
        cost_estimate=pl.CostEstimate(
            flops=ITERS * 8 * COLS * 1536 * ROWS, bytes_accessed=4 * 2**20, transcendentals=0
        ),
    )(green.reshape(2, COLS, ROWS), hamiltonian, interaction)
    return result.reshape(shape)


def solution(mesh):
    in_specs = (P(None, None, "tp", None, "ta"), P(), P())
    out_specs = P(None, None, "tp", None, "ta")
    return jax.shard_map(shards, mesh=mesh, in_specs=in_specs, out_specs=out_specs, check_vma=False)
```

```python
import functools

import jax
import jax.numpy as jnp
from jax import lax
from jax.experimental import pallas as pl
from jax.experimental.pallas import tpu as pltpu
from jax.sharding import PartitionSpec as P

NO = 32
ITERS = 2
N_TA = 8
N_TP = 32
N_Y = 4
N_Z = 4
STRIPE = 16
ROWS = 512
COLS = 128
FACTOR = 1.0 / 32.0
PIECES = ((1, 2, 0, 256), (0, 1, 0, 128), (5, 1, 128, 128))

MESH = pl.DeviceIdType.MESH
HIGHEST = lax.Precision.HIGHEST
F32 = jnp.float32
BF16 = jnp.bfloat16


def iota(shape, dim):
    return lax.broadcasted_iota(jnp.int32, shape, dim)


def exact_dot(left, right, contract=((1,), (0,))):
    return lax.dot_general(
        left, right, (contract, ((), ())), precision=HIGHEST, preferred_element_type=F32
    )


def kernel(
    green_hbm,
    ham_hbm,
    inter_hbm,
    out_ref,
    green_ref,
    ham_ref,
    inter_ref,
    rounded,
    previous,
    earliest,
    stage_out,
    stage_in,
    mirror_out,
    mirror_in,
    flipped,
    window,
    straight,
    crossed,
    total,
    hamilton,
    weights,
    blocked,
    row_send,
    row_recv,
    stage_send,
    stage_recv,
    mirror_send,
    mirror_recv,
    window_send,
    window_recv,
    input_sem,
):
    ta = lax.axis_index("ta")
    tp = lax.axis_index("tp")
    y = tp // 8
    zl = lax.rem(tp // 2, 4)
    core = lax.rem(tp, 2)

    def ta_plus(k):
        return lax.rem(ta + k + N_TA, N_TA)

    near = zl + 1 - 2 * lax.rem(zl, 2)
    middle = 2 - zl // 2
    far = 3 * (1 - zl // 2)
    z_order = (zl, near, middle, far)

    def stripe_of(q):
        return pl.ds(pl.multiple_of(q * STRIPE, STRIPE), STRIPE)

    def place(dy, z, c):
        return lax.rem(y + dy, N_Y) * 8 + z * 2 + c

    inputs = [
        pltpu.make_async_copy(src, dst, input_sem.at[n])
        for n, (src, dst) in enumerate(
            ((green_hbm, green_ref), (ham_hbm, ham_ref), (inter_hbm, inter_ref))
        )
    ]
    for copy in inputs:
        copy.start()

    barrier = pltpu.get_barrier_semaphore()

    for dy in (1, 2, 3):
        pl.semaphore_signal(
            barrier, inc=1, device_id=(ta, place(dy, zl, core)), device_id_type=MESH
        )
    for k in (1, 2, 0):
        for z in (far, middle, near, zl):
            for other in (1, 0):
                if k == 0 and z is zl and other == 0:
                    continue
                c = 1 - core if other else core
                pl.semaphore_signal(
                    barrier,
                    inc=1,
                    device_id=(ta_plus(-k), place(0, z, c)),
                    device_id_type=MESH,
                )

    def remote(src, dst, send, recv, target):
        return pltpu.make_async_remote_copy(
            src_ref=src,
            dst_ref=dst,
            send_sem=send,
            recv_sem=recv,
            device_id=target,
            device_id_type=MESH,
        )

    def build_stage(state, it):
        for k in range(3):
            group = pl.multiple_of(ta_plus(k) * STRIPE, STRIPE)
            for r in range(2):
                piece = state[r, pl.ds(group, STRIPE), :].astype(BF16)
                for j in range(N_Y):
                    stage_out[it, j, pl.ds((2 * k + r) * STRIPE, STRIPE), :] = piece[
                        :, j * 128 : (j + 1) * 128
                    ]

    def build_rounded(state, it):
        for r in range(2):
            rounded[it, pl.ds(r * COLS, COLS), :] = state[r].astype(BF16)

    def row_copy(it, n):
        k, start, count = PIECES[n][1:]
        return remote(
            rounded.at[it, pl.ds(start, count)],
            (previous if k == 1 else earliest).at[it, pl.ds(start, count)],
            row_send.at[it, n],
            row_recv.at[it, n],
            (ta_plus(k), tp),
        )

    def stage_copy(it, dy):
        j = lax.rem(y + dy, N_Y)
        return remote(
            stage_out.at[it, j],
            stage_in.at[it, y],
            stage_send.at[it, dy - 1],
            stage_recv.at[it, dy - 1],
            (ta, place(dy, zl, core)),
        )

    def build_mirror(it):
        stage_in[it, y] = stage_out[it, y]
        for k in (1, 2, 0):
            stacked = jnp.concatenate(
                [stage_in[it, j, pl.ds(2 * k * STRIPE, 2 * STRIPE), :] for j in range(N_Y)],
                axis=0,
            )
            mirror_out[it, k] = stacked.astype(F32).T.astype(BF16)
            send_mirror(it, k)
        own = stripe_of(zl * 2 + core)
        mirror_in[it, 0, own, :] = mirror_out[it, 0, own, :]

    def send_mirror(it, k):
        for z in (far, middle, near, zl):
            for other in (1, 0):
                if k == 0 and z is zl and other == 0:
                    continue
                c = 1 - core if other else core
                remote(
                    mirror_out.at[it, k, stripe_of(z * 2 + c), :],
                    mirror_in.at[it, k, stripe_of(zl * 2 + core), :],
                    mirror_send.at[it, k],
                    mirror_recv.at[it, k],
                    (ta_plus(k), place(0, z, c)),
                ).start()

    def mirror_bytes(ref, it, k):
        return ref.at[it, k] if k else ref.at[it, 0, pl.ds(0, 7 * STRIPE), :]

    def wait_bytes(ref, sem):
        pltpu.make_async_copy(ref, ref, sem).wait()

    def flip(it, k):
        piece = iota((STRIPE, 128), 1) // STRIPE
        parts = [
            mirror_in[it, k, pl.ds(i * STRIPE, STRIPE), :].astype(F32) for i in range(8)
        ]
        for bit in (1, 2, 4):
            low = (piece // bit) % 2 == 0
            for i in range(8):
                if i & bit:
                    continue
                first, second = parts[i], parts[i | bit]
                parts[i] = jnp.where(low, first, pltpu.roll(second, STRIPE * bit, 1))
                parts[i | bit] = jnp.where(
                    low, pltpu.roll(first, 128 - STRIPE * bit, 1), second
                )
        for j in range(N_Y):
            for r in range(2):
                flipped[k, r, :, pl.ds(j * 128, 128)] = parts[2 * j + r]

    def column(state, r, k):
        group = pl.multiple_of(ta_plus(-k) * STRIPE, STRIPE)
        return state[r, pl.ds(group, STRIPE), :]

    def self_energy(it, kind, real, imag, mirror_real, mirror_imag):
        real_square = real * real - imag * imag
        imag_square = 2.0 * real * imag
        coupling = weights[...]
        window[it, 2 * kind, y, zl, core] = (
            coupling * (real_square * mirror_real - imag_square * mirror_imag)
        ).astype(BF16)
        window[it, 2 * kind + 1, y, zl, core] = (
            coupling * (real_square * mirror_imag + imag_square * mirror_real)
        ).astype(BF16)

    def sigma_combined(state, it):
        later = iota((STRIPE, ROWS), 1) // NO < tp // 2
        real, imag = (
            jnp.where(later, column(state, r, 2), column(state, r, 0)) for r in range(2)
        )
        mirror_real, mirror_imag = (
            jnp.where(later, flipped[2, r], flipped[0, r]) for r in range(2)
        )
        self_energy(it, 0, real, imag, mirror_real, mirror_imag)

    def sigma_middle(state, it):
        self_energy(
            it, 1, column(state, 0, 1), column(state, 1, 1), flipped[1, 0], flipped[1, 1]
        )

    def send_own(it, kind):
        part = window.at[it, pl.ds(2 * kind, 2), y, :, core]
        for z in (near, middle, far):
            remote(
                part.at[:, zl],
                part.at[:, zl],
                window_send.at[it],
                window_recv.at[it, kind, zl],
                (ta, place(0, z, core)),
            ).start()

    def wait_z(it, kind, z):
        part = window.at[it, pl.ds(2 * kind, 2), y, :, core]
        wait_bytes(part.at[:, z], window_recv.at[it, kind, z])

    def y_part(it, kind, dy, piece):
        part = window.at[it, pl.ds(2 * kind, 2), lax.rem(y + dy, N_Y)]
        return part.at[:, z_order[piece], core]

    def y_copy(it, kind, piece, source, target):
        part = y_part(it, kind, source, piece)
        return remote(
            part,
            part,
            window_send.at[it],
            window_recv.at[it, kind, 4 + 4 * piece + lax.rem(y + source, N_Y)],
            (ta, place(target, zl, core)),
        )

    def send_y(it, kind, piece):
        for dy in (2, 1, 3) if piece == 3 else (1, 3):
            y_copy(it, kind, piece, 0, dy).start()

    def wait_y(it, kind, piece, dy):
        wait_bytes(
            y_part(it, kind, dy, piece),
            window_recv.at[it, kind, 4 + 4 * piece + lax.rem(y + dy, N_Y)],
        )

    def relay(it, kind, piece):
        source, target = ((3, 1), (1, 3))[kind]
        wait_y(it, kind, piece, source)
        y_copy(it, kind, piece, source, target).start()

    def send_sibling(it, kind, dy):
        j = lax.rem(y + dy, N_Y)
        part = window.at[it, pl.ds(2 * kind, 2), j, :, core]
        remote(
            part,
            part,
            window_send.at[it],
            window_recv.at[it, kind, 20 + j],
            (ta, place(0, zl, 1 - core)),
        ).start()

    def wait_sibling(it, kind, dy):
        j = lax.rem(y + dy, N_Y)
        wait_bytes(
            window.at[it, pl.ds(2 * kind, 2), j, :, 1 - core], window_recv.at[it, kind, 20 + j]
        )

    def last_part(it, kind, pair, c):
        j = lax.rem(y + 2, N_Y)
        return window.at[it, pl.ds(2 * kind, 2), j, pl.ds(2 * pair, 2), c]

    def pass_last(it, kind):
        for half in range(2):
            pair = zl // 2 if half == 0 else 1 - zl // 2
            for piece in (2 * half, 2 * half + 1):
                wait_y(it, kind, piece, 2)
            part = last_part(it, kind, pair, core)
            remote(
                part,
                part,
                window_send.at[it],
                window_recv.at[it, kind, 24 + half],
                (ta, place(0, zl, 1 - core)),
            ).start()

    def wait_last(it, kind):
        for half in range(2):
            pair = zl // 2 if half == 0 else 1 - zl // 2
            wait_bytes(last_part(it, kind, pair, 1 - core), window_recv.at[it, kind, 24 + half])

    def lefts(it, which, source, keep):
        for r in range(2):
            half = source[it, pl.ds(r * COLS, COLS), :]
            if keep is not None:
                half = jnp.where(keep, half, jnp.zeros_like(half))
            straight[which, pl.ds(r * COLS, COLS), :] = half
            crossed[which, pl.ds((1 - r) * COLS, COLS), :] = -half if r == 1 else half

    def rows_of(it, part, j):
        return window[it, part, j].reshape(128, ROWS)

    def multiply_combined(it, dy):
        j = lax.rem(y + dy, N_Y)
        lanes = pl.ds(pl.multiple_of(j * 128, 128), 128)
        later = (j * 4 + iota((128, ROWS), 0) // NO) > iota((128, ROWS), 1) // NO
        old = jnp.where(later, 1.0, 0.0).astype(BF16)
        new = jnp.where(later, 0.0, 1.0).astype(BF16)
        left_parts, right_parts = [], []
        for r, side in ((0, straight), (1, crossed)):
            combined = rows_of(it, r, j)
            right_parts += [combined * new, combined * old]
            left_parts += [side[which, :, lanes] for which in range(2)]
        product = jnp.dot(
            jnp.concatenate(left_parts, axis=1),
            jnp.concatenate(right_parts, axis=0),
            preferred_element_type=F32,
        )
        if dy == 0:
            total[...] = product
        else:
            total[...] += product

    def multiply_middle(it, r):
        left = previous[it, pl.ds(r * COLS, COLS), :]
        left = jnp.where(ta >= 1, left, jnp.zeros_like(left))
        with_real, with_imag = (
            jnp.dot(
                left, window[it, 2 + part].reshape(ROWS, ROWS), preferred_element_type=F32
            )
            for part in range(2)
        )
        top, bottom = pl.ds(0, COLS), pl.ds(COLS, COLS)
        if r == 0:
            total[top, :] += with_real
            total[bottom, :] += with_imag
        else:
            total[top, :] -= with_imag
            total[bottom, :] += with_real

    def hamilton_term(state):
        for r in range(2):
            for b in range(4):
                lanes = pl.ds(b * 128, 128)
                hamilton[pl.ds(r * COLS, COLS), lanes] = exact_dot(
                    state[r, :, lanes], blocked[...]
                )

    def prepare():
        squared = inter_ref[...] * inter_ref[...]
        pick = (iota((STRIPE, NO), 1) == core * STRIPE + iota((STRIPE, NO), 0)).astype(F32)
        picked = exact_dot(pick, squared, ((1,), (1,)))
        spread = (lax.rem(iota((NO, ROWS), 1), NO) == iota((NO, ROWS), 0)).astype(F32)
        weights[...] = exact_dot(picked, spread)
        tall = (lax.rem(iota((128, NO), 0), NO) == iota((128, NO), 1)).astype(F32)
        wide = (lax.rem(iota((NO, 128), 1), NO) == iota((NO, 128), 0)).astype(F32)
        across = exact_dot(exact_dot(tall, ham_ref[...], ((1,), (1,))), wide)
        same = iota((128, 128), 0) // NO == iota((128, 128), 1) // NO
        blocked[...] = jnp.where(same, across, 0.0)

    for copy in inputs:
        copy.wait()
    build_stage(green_ref, 0)
    pl.semaphore_wait(barrier, 26)

    started = []
    for it in range(ITERS):
        state = green_ref if it == 0 else out_ref
        if it:
            build_stage(state, it)
        stages = [stage_copy(it, dy) for dy in (1, 2, 3)]
        for n in (1, 0, 2):
            stages[n].start()
        build_rounded(state, it)
        rows = [row_copy(it, n) for n in range(len(PIECES))]

        def start_rows(stage):
            for piece, copy in zip(PIECES, rows):
                if piece[0] == stage:
                    copy.start()

        def wait_rows(k):
            for piece, copy in zip(PIECES, rows):
                if piece[1] == k:
                    copy.wait_recv()

        start_rows(0)
        if it == 0:
            prepare()
        lefts(it, 0, rounded, None)
        for copy in stages:
            copy.wait_recv()
        build_mirror(it)
        start_rows(1)
        hamilton_term(state)
        for k in (0, 2):
            wait_bytes(mirror_bytes(mirror_in, it, k), mirror_recv.at[it, k])
            flip(it, k)
        sigma_combined(state, it)
        send_own(it, 0)
        send_y(it, 0, 0)
        start_rows(3)
        wait_bytes(mirror_bytes(mirror_in, it, 1), mirror_recv.at[it, 1])
        flip(it, 1)
        sigma_middle(state, it)
        send_own(it, 1)
        send_y(it, 1, 0)
        start_rows(4)
        for kind in range(2):
            wait_z(it, kind, near)
            send_y(it, kind, 1)
        for kind in range(2):
            relay(it, kind, 0)
        for kind in range(2):
            wait_z(it, kind, middle)
            send_y(it, kind, 2)
        for kind in range(2):
            relay(it, kind, 1)
        for kind in range(2):
            wait_z(it, kind, far)
            send_y(it, kind, 3)
            send_sibling(it, kind, 0)
        start_rows(5)
        for kind in range(2):
            relay(it, kind, 2)
        for kind in range(2):
            dy = 3 if kind == 0 else 1
            wait_y(it, kind, 3, dy)
            send_sibling(it, kind, dy)
        for kind in range(2):
            dy = 1 if kind == 0 else 3
            for piece in range(4):
                wait_y(it, kind, piece, dy)
            send_sibling(it, kind, dy)
        wait_rows(2)
        lefts(it, 1, earliest, ta >= 2)
        wait_sibling(it, 0, 0)
        multiply_combined(it, 0)
        pass_last(it, 0)
        for dy in (3, 1):
            wait_sibling(it, 0, dy)
            multiply_combined(it, dy)
        pass_last(it, 1)
        wait_last(it, 0)
        multiply_combined(it, 2)
        for dy in (0, 1, 3):
            wait_sibling(it, 1, dy)
        wait_last(it, 1)
        for r in range(2):
            rows[1 + r].wait_recv()
            multiply_middle(it, r)
        out_real = state[0] + 0.5 * (
            hamilton[pl.ds(COLS, COLS), :] + FACTOR * total[pl.ds(COLS, COLS), :]
        )
        out_imag = state[1] - 0.5 * (
            hamilton[pl.ds(0, COLS), :] + FACTOR * total[pl.ds(0, COLS), :]
        )
        out_ref[0] = out_real
        out_ref[1] = out_imag
        started.append(rows + stages)

    for it in range(ITERS):
        for k in range(3):
            wait_bytes(mirror_bytes(mirror_out, it, k), mirror_send.at[it, k])
        for copy in started[it]:
            copy.wait_send()
        wait_bytes(window.at[it, :, pl.ds(0, 3)], window_send.at[it])
        wait_bytes(window.at[it, :, 3, pl.ds(0, 3)], window_send.at[it])
        wait_bytes(window.at[it, :, 3, 3, 0], window_send.at[it])


def shards(green, hamiltonian, interaction):
    shape = green.shape
    whole = pl.BlockSpec(memory_space=pltpu.VMEM)
    dma = pltpu.SemaphoreType.DMA
    result = pl.pallas_call(
        kernel,
        out_shape=jax.ShapeDtypeStruct((2, COLS, ROWS), F32),
        in_specs=[pl.BlockSpec(memory_space=pltpu.HBM)] * 3,
        out_specs=whole,
        scratch_shapes=[
            pltpu.VMEM((2, COLS, ROWS), F32),
            pltpu.VMEM((NO, NO), F32),
            pltpu.VMEM((NO, NO), F32),
            pltpu.VMEM((ITERS, 2 * COLS, ROWS), BF16),
            pltpu.VMEM((ITERS, 2 * COLS, ROWS), BF16),
            pltpu.VMEM((ITERS, 2 * COLS, ROWS), BF16),
            pltpu.VMEM((ITERS, N_Y, 6 * STRIPE, 128), BF16),
            pltpu.VMEM((ITERS, N_Y, 6 * STRIPE, 128), BF16),
            pltpu.VMEM((ITERS, 3, 128, 128), BF16),
            pltpu.VMEM((ITERS, 3, 128, 128), BF16),
            pltpu.VMEM((3, 2, STRIPE, ROWS), F32),
            pltpu.VMEM((ITERS, 4, N_Y, N_Z, 2, STRIPE, ROWS), BF16),
            pltpu.VMEM((2, 2 * COLS, ROWS), BF16),
            pltpu.VMEM((2, 2 * COLS, ROWS), BF16),
            pltpu.VMEM((2 * COLS, ROWS), F32),
            pltpu.VMEM((2 * COLS, ROWS), F32),
            pltpu.VMEM((STRIPE, ROWS), F32),
            pltpu.VMEM((128, 128), F32),
            dma((ITERS, len(PIECES))),
            dma((ITERS, len(PIECES))),
            dma((ITERS, 3)),
            dma((ITERS, 3)),
            dma((ITERS, 3)),
            dma((ITERS, 3)),
            dma((ITERS,)),
            dma((ITERS, 2, 26)),
            dma((3,)),
        ],
        compiler_params=pltpu.CompilerParams(
            collective_id=0, has_side_effects=True, vmem_limit_bytes=63 * 2**20 + 900000
        ),
        cost_estimate=pl.CostEstimate(
            flops=ITERS * 8 * COLS * 1536 * ROWS, bytes_accessed=4 * 2**20, transcendentals=0
        ),
    )(green.reshape(2, COLS, ROWS), hamiltonian, interaction)
    return result.reshape(shape)


def solution(mesh):
    in_specs = (P(None, None, "tp", None, "ta"), P(), P())
    out_specs = P(None, None, "tp", None, "ta")
    return jax.shard_map(shards, mesh=mesh, in_specs=in_specs, out_specs=out_specs, check_vma=False)
```

```python
import functools

import jax
import jax.numpy as jnp
from jax import lax
from jax.experimental import pallas as pl
from jax.experimental.pallas import tpu as pltpu
from jax.sharding import PartitionSpec as P

NO = 32
ITERS = 2
N_TA = 8
N_TP = 32
N_Y = 4
N_Z = 4
STRIPE = 16
ROWS = 512
COLS = 128
FACTOR = 1.0 / 32.0
PIECES = ((1, 2, 0, 256), (0, 1, 0, 128), (5, 1, 128, 128))

MESH = pl.DeviceIdType.MESH
HIGHEST = lax.Precision.HIGHEST
F32 = jnp.float32
BF16 = jnp.bfloat16


def iota(shape, dim):
    return lax.broadcasted_iota(jnp.int32, shape, dim)


def exact_dot(left, right, contract=((1,), (0,))):
    return lax.dot_general(
        left, right, (contract, ((), ())), precision=HIGHEST, preferred_element_type=F32
    )


def kernel(
    green_hbm,
    orbital_hbm,
    out_ref,
    green_ref,
    orbital_ref,
    rounded,
    previous,
    earliest,
    stage_out,
    stage_in,
    mirror_out,
    mirror_in,
    flipped,
    window,
    straight,
    crossed,
    total,
    hamilton,
    weights,
    blocked,
    row_send,
    row_recv,
    stage_send,
    stage_recv,
    mirror_send,
    mirror_recv,
    window_send,
    window_recv,
    input_sem,
):
    ta = lax.axis_index("ta")
    tp = lax.axis_index("tp")
    y = tp // 8
    zl = lax.rem(tp // 2, 4)
    core = lax.rem(tp, 2)

    def ta_plus(k):
        return lax.rem(ta + k + N_TA, N_TA)

    near = zl + 1 - 2 * lax.rem(zl, 2)
    middle = 2 - zl // 2
    far = 3 * (1 - zl // 2)
    z_order = (zl, near, middle, far)

    def stripe_of(q):
        return pl.ds(pl.multiple_of(q * STRIPE, STRIPE), STRIPE)

    def place(dy, z, c):
        return lax.rem(y + dy, N_Y) * 8 + z * 2 + c

    inputs = [
        pltpu.make_async_copy(src, dst, input_sem.at[n])
        for n, (src, dst) in enumerate(
            ((green_hbm, green_ref), (orbital_hbm, orbital_ref))
        )
    ]
    for copy in inputs:
        copy.start()

    barrier = pltpu.get_barrier_semaphore()

    for dy in (1, 2, 3):
        pl.semaphore_signal(
            barrier, inc=1, device_id=(ta, place(dy, zl, core)), device_id_type=MESH
        )
    for k in (1, 2, 0):
        for z in (far, middle, near, zl):
            for other in (1, 0):
                if k == 0 and z is zl and other == 0:
                    continue
                c = 1 - core if other else core
                pl.semaphore_signal(
                    barrier,
                    inc=1,
                    device_id=(ta_plus(-k), place(0, z, c)),
                    device_id_type=MESH,
                )

    def remote(src, dst, send, recv, target):
        return pltpu.make_async_remote_copy(
            src_ref=src,
            dst_ref=dst,
            send_sem=send,
            recv_sem=recv,
            device_id=target,
            device_id_type=MESH,
        )

    def build_stage(state, it):
        for k in range(3):
            group = pl.multiple_of(ta_plus(k) * STRIPE, STRIPE)
            for r in range(2):
                piece = state[r, pl.ds(group, STRIPE), :].astype(BF16)
                for j in range(N_Y):
                    stage_out[it, j, pl.ds((2 * k + r) * STRIPE, STRIPE), :] = piece[
                        :, j * 128 : (j + 1) * 128
                    ]

    def build_rounded(state, it):
        for r in range(2):
            rounded[it, pl.ds(r * COLS, COLS), :] = state[r].astype(BF16)

    def row_copy(it, n):
        k, start, count = PIECES[n][1:]
        return remote(
            rounded.at[it, pl.ds(start, count)],
            (previous if k == 1 else earliest).at[it, pl.ds(start, count)],
            row_send.at[it, n],
            row_recv.at[it, n],
            (ta_plus(k), tp),
        )

    def stage_copy(it, dy):
        j = lax.rem(y + dy, N_Y)
        return remote(
            stage_out.at[it, j],
            stage_in.at[it, y],
            stage_send.at[it, dy - 1],
            stage_recv.at[it, dy - 1],
            (ta, place(dy, zl, core)),
        )

    def build_mirror(it):
        stage_in[it, y] = stage_out[it, y]
        for k in (1, 2, 0):
            stacked = jnp.concatenate(
                [stage_in[it, j, pl.ds(2 * k * STRIPE, 2 * STRIPE), :] for j in range(N_Y)],
                axis=0,
            )
            mirror_out[it, k] = stacked.astype(F32).T.astype(BF16)
            send_mirror(it, k)
        own = stripe_of(zl * 2 + core)
        mirror_in[it, 0, own, :] = mirror_out[it, 0, own, :]

    def send_mirror(it, k):
        for z in (far, middle, near, zl):
            for other in (1, 0):
                if k == 0 and z is zl and other == 0:
                    continue
                c = 1 - core if other else core
                remote(
                    mirror_out.at[it, k, stripe_of(z * 2 + c), :],
                    mirror_in.at[it, k, stripe_of(zl * 2 + core), :],
                    mirror_send.at[it, k],
                    mirror_recv.at[it, k],
                    (ta_plus(k), place(0, z, c)),
                ).start()

    def mirror_bytes(ref, it, k):
        return ref.at[it, k] if k else ref.at[it, 0, pl.ds(0, 7 * STRIPE), :]

    def wait_bytes(ref, sem):
        pltpu.make_async_copy(ref, ref, sem).wait()

    def flip(it, k):
        piece = iota((STRIPE, 128), 1) // STRIPE
        parts = [
            mirror_in[it, k, pl.ds(i * STRIPE, STRIPE), :].astype(F32) for i in range(8)
        ]
        for bit in (1, 2, 4):
            low = (piece // bit) % 2 == 0
            for i in range(8):
                if i & bit:
                    continue
                first, second = parts[i], parts[i | bit]
                parts[i] = jnp.where(low, first, pltpu.roll(second, STRIPE * bit, 1))
                parts[i | bit] = jnp.where(
                    low, pltpu.roll(first, 128 - STRIPE * bit, 1), second
                )
        for j in range(N_Y):
            for r in range(2):
                flipped[k, r, :, pl.ds(j * 128, 128)] = parts[2 * j + r]

    def column(state, r, k):
        group = pl.multiple_of(ta_plus(-k) * STRIPE, STRIPE)
        return state[r, pl.ds(group, STRIPE), :]

    def self_energy(it, kind, real, imag, mirror_real, mirror_imag):
        real_square = real * real - imag * imag
        imag_square = 2.0 * real * imag
        coupling = weights[...]
        window[it, 2 * kind, y, zl, core] = (
            coupling * (real_square * mirror_real - imag_square * mirror_imag)
        ).astype(BF16)
        window[it, 2 * kind + 1, y, zl, core] = (
            coupling * (real_square * mirror_imag + imag_square * mirror_real)
        ).astype(BF16)

    def sigma_combined(state, it):
        later = iota((STRIPE, ROWS), 1) // NO < tp // 2
        real, imag = (
            jnp.where(later, column(state, r, 2), column(state, r, 0)) for r in range(2)
        )
        mirror_real, mirror_imag = (
            jnp.where(later, flipped[2, r], flipped[0, r]) for r in range(2)
        )
        self_energy(it, 0, real, imag, mirror_real, mirror_imag)

    def sigma_middle(state, it):
        self_energy(
            it, 1, column(state, 0, 1), column(state, 1, 1), flipped[1, 0], flipped[1, 1]
        )

    def send_own(it, kind):
        part = window.at[it, pl.ds(2 * kind, 2), y, :, core]
        for z in (near, middle, far):
            remote(
                part.at[:, zl],
                part.at[:, zl],
                window_send.at[it],
                window_recv.at[it, kind, zl],
                (ta, place(0, z, core)),
            ).start()

    def wait_z(it, kind, z):
        part = window.at[it, pl.ds(2 * kind, 2), y, :, core]
        wait_bytes(part.at[:, z], window_recv.at[it, kind, z])

    def y_part(it, kind, dy, piece):
        part = window.at[it, pl.ds(2 * kind, 2), lax.rem(y + dy, N_Y)]
        return part.at[:, z_order[piece], core]

    def y_copy(it, kind, piece, source, target):
        part = y_part(it, kind, source, piece)
        return remote(
            part,
            part,
            window_send.at[it],
            window_recv.at[it, kind, 4 + 4 * piece + lax.rem(y + source, N_Y)],
            (ta, place(target, zl, core)),
        )

    def send_y(it, kind, piece):
        for dy in (2, 1, 3) if piece == 3 else (1, 3):
            y_copy(it, kind, piece, 0, dy).start()

    def wait_y(it, kind, piece, dy):
        wait_bytes(
            y_part(it, kind, dy, piece),
            window_recv.at[it, kind, 4 + 4 * piece + lax.rem(y + dy, N_Y)],
        )

    def relay(it, kind, piece):
        source, target = ((3, 1), (1, 3))[kind]
        wait_y(it, kind, piece, source)
        y_copy(it, kind, piece, source, target).start()

    def send_sibling(it, kind, dy):
        j = lax.rem(y + dy, N_Y)
        part = window.at[it, pl.ds(2 * kind, 2), j, :, core]
        remote(
            part,
            part,
            window_send.at[it],
            window_recv.at[it, kind, 20 + j],
            (ta, place(0, zl, 1 - core)),
        ).start()

    def wait_sibling(it, kind, dy):
        j = lax.rem(y + dy, N_Y)
        wait_bytes(
            window.at[it, pl.ds(2 * kind, 2), j, :, 1 - core], window_recv.at[it, kind, 20 + j]
        )

    def last_part(it, kind, pair, c):
        j = lax.rem(y + 2, N_Y)
        return window.at[it, pl.ds(2 * kind, 2), j, pl.ds(2 * pair, 2), c]

    def pass_last(it, kind):
        for half in range(2):
            pair = zl // 2 if half == 0 else 1 - zl // 2
            for piece in (2 * half, 2 * half + 1):
                wait_y(it, kind, piece, 2)
            part = last_part(it, kind, pair, core)
            remote(
                part,
                part,
                window_send.at[it],
                window_recv.at[it, kind, 24 + half],
                (ta, place(0, zl, 1 - core)),
            ).start()

    def wait_last(it, kind):
        for half in range(2):
            pair = zl // 2 if half == 0 else 1 - zl // 2
            wait_bytes(last_part(it, kind, pair, 1 - core), window_recv.at[it, kind, 24 + half])

    def lefts(it, which, source, keep):
        for r in range(2):
            half = source[it, pl.ds(r * COLS, COLS), :]
            if keep is not None:
                half = jnp.where(keep, half, jnp.zeros_like(half))
            straight[which, pl.ds(r * COLS, COLS), :] = half
            crossed[which, pl.ds((1 - r) * COLS, COLS), :] = -half if r == 1 else half

    def rows_of(it, part, j):
        return window[it, part, j].reshape(128, ROWS)

    def multiply_combined(it, dy):
        j = lax.rem(y + dy, N_Y)
        lanes = pl.ds(pl.multiple_of(j * 128, 128), 128)
        later = (j * 4 + iota((128, ROWS), 0) // NO) > iota((128, ROWS), 1) // NO
        old = jnp.where(later, 1.0, 0.0).astype(BF16)
        new = jnp.where(later, 0.0, 1.0).astype(BF16)
        left_parts, right_parts = [], []
        for r, side in ((0, straight), (1, crossed)):
            combined = rows_of(it, r, j)
            right_parts += [combined * new, combined * old]
            left_parts += [side[which, :, lanes] for which in range(2)]
        product = jnp.dot(
            jnp.concatenate(left_parts, axis=1),
            jnp.concatenate(right_parts, axis=0),
            preferred_element_type=F32,
        )
        if dy == 0:
            total[...] = product
        else:
            total[...] += product

    def multiply_middle(it, r):
        left = previous[it, pl.ds(r * COLS, COLS), :]
        left = jnp.where(ta >= 1, left, jnp.zeros_like(left))
        with_real, with_imag = (
            jnp.dot(
                left, window[it, 2 + part].reshape(ROWS, ROWS), preferred_element_type=F32
            )
            for part in range(2)
        )
        top, bottom = pl.ds(0, COLS), pl.ds(COLS, COLS)
        if r == 0:
            total[top, :] += with_real
            total[bottom, :] += with_imag
        else:
            total[top, :] -= with_imag
            total[bottom, :] += with_real

    def hamilton_term(state):
        for r in range(2):
            for b in range(4):
                lanes = pl.ds(b * 128, 128)
                hamilton[pl.ds(r * COLS, COLS), lanes] = exact_dot(
                    state[r, :, lanes], blocked[...]
                )

    def prepare():
        squared = orbital_ref[1] * orbital_ref[1]
        pick = (iota((STRIPE, NO), 1) == core * STRIPE + iota((STRIPE, NO), 0)).astype(F32)
        picked = exact_dot(pick, squared, ((1,), (1,)))
        spread = (lax.rem(iota((NO, ROWS), 1), NO) == iota((NO, ROWS), 0)).astype(F32)
        weights[...] = exact_dot(picked, spread)
        tall = (lax.rem(iota((128, NO), 0), NO) == iota((128, NO), 1)).astype(F32)
        wide = (lax.rem(iota((NO, 128), 1), NO) == iota((NO, 128), 0)).astype(F32)
        across = exact_dot(exact_dot(tall, orbital_ref[0], ((1,), (1,))), wide)
        same = iota((128, 128), 0) // NO == iota((128, 128), 1) // NO
        blocked[...] = jnp.where(same, across, 0.0)

    for copy in inputs:
        copy.wait()
    build_stage(green_ref, 0)
    pl.semaphore_wait(barrier, 26)

    started = []
    for it in range(ITERS):
        state = green_ref if it == 0 else out_ref
        if it:
            build_stage(state, it)
        stages = [stage_copy(it, dy) for dy in (1, 2, 3)]
        for n in (1, 0, 2):
            stages[n].start()
        build_rounded(state, it)
        rows = [row_copy(it, n) for n in range(len(PIECES))]

        def start_rows(stage):
            for piece, copy in zip(PIECES, rows):
                if piece[0] == stage:
                    copy.start()

        def wait_rows(k):
            for piece, copy in zip(PIECES, rows):
                if piece[1] == k:
                    copy.wait_recv()

        start_rows(0)
        if it == 0:
            prepare()
        lefts(it, 0, rounded, None)
        for copy in stages:
            copy.wait_recv()
        build_mirror(it)
        start_rows(1)
        hamilton_term(state)
        for k in (0, 2):
            wait_bytes(mirror_bytes(mirror_in, it, k), mirror_recv.at[it, k])
            flip(it, k)
        sigma_combined(state, it)
        send_own(it, 0)
        send_y(it, 0, 0)
        start_rows(3)
        wait_bytes(mirror_bytes(mirror_in, it, 1), mirror_recv.at[it, 1])
        flip(it, 1)
        sigma_middle(state, it)
        send_own(it, 1)
        send_y(it, 1, 0)
        start_rows(4)
        for kind in range(2):
            wait_z(it, kind, near)
            send_y(it, kind, 1)
        for kind in range(2):
            relay(it, kind, 0)
        for kind in range(2):
            wait_z(it, kind, middle)
            send_y(it, kind, 2)
        for kind in range(2):
            relay(it, kind, 1)
        for kind in range(2):
            wait_z(it, kind, far)
            send_y(it, kind, 3)
            send_sibling(it, kind, 0)
        start_rows(5)
        for kind in range(2):
            relay(it, kind, 2)
        for kind in range(2):
            dy = 3 if kind == 0 else 1
            wait_y(it, kind, 3, dy)
            send_sibling(it, kind, dy)
        for kind in range(2):
            dy = 1 if kind == 0 else 3
            for piece in range(4):
                wait_y(it, kind, piece, dy)
            send_sibling(it, kind, dy)
        wait_rows(2)
        lefts(it, 1, earliest, ta >= 2)
        wait_sibling(it, 0, 0)
        multiply_combined(it, 0)
        pass_last(it, 0)
        for dy in (3, 1):
            wait_sibling(it, 0, dy)
            multiply_combined(it, dy)
        pass_last(it, 1)
        wait_last(it, 0)
        multiply_combined(it, 2)
        for dy in (0, 1, 3):
            wait_sibling(it, 1, dy)
        wait_last(it, 1)
        for r in range(2):
            rows[1 + r].wait_recv()
            multiply_middle(it, r)
        out_real = state[0] + 0.5 * (
            hamilton[pl.ds(COLS, COLS), :] + FACTOR * total[pl.ds(COLS, COLS), :]
        )
        out_imag = state[1] - 0.5 * (
            hamilton[pl.ds(0, COLS), :] + FACTOR * total[pl.ds(0, COLS), :]
        )
        out_ref[0] = out_real
        out_ref[1] = out_imag
        started.append(rows + stages)

    for it in range(ITERS):
        for k in range(3):
            wait_bytes(mirror_bytes(mirror_out, it, k), mirror_send.at[it, k])
        for copy in started[it]:
            copy.wait_send()
        wait_bytes(window.at[it, :, pl.ds(0, 3)], window_send.at[it])
        wait_bytes(window.at[it, :, 3, pl.ds(0, 3)], window_send.at[it])
        wait_bytes(window.at[it, :, 3, 3, 0], window_send.at[it])


def shards(green, hamiltonian, interaction):
    shape = green.shape
    whole = pl.BlockSpec(memory_space=pltpu.VMEM)
    dma = pltpu.SemaphoreType.DMA
    result = pl.pallas_call(
        kernel,
        out_shape=jax.ShapeDtypeStruct((2, COLS, ROWS), F32),
        in_specs=[pl.BlockSpec(memory_space=pltpu.HBM)] * 2,
        out_specs=whole,
        scratch_shapes=[
            pltpu.VMEM((2, COLS, ROWS), F32),
            pltpu.VMEM((2, NO, NO), F32),
            pltpu.VMEM((ITERS, 2 * COLS, ROWS), BF16),
            pltpu.VMEM((ITERS, 2 * COLS, ROWS), BF16),
            pltpu.VMEM((ITERS, 2 * COLS, ROWS), BF16),
            pltpu.VMEM((ITERS, N_Y, 6 * STRIPE, 128), BF16),
            pltpu.VMEM((ITERS, N_Y, 6 * STRIPE, 128), BF16),
            pltpu.VMEM((ITERS, 3, 128, 128), BF16),
            pltpu.VMEM((ITERS, 3, 128, 128), BF16),
            pltpu.VMEM((3, 2, STRIPE, ROWS), F32),
            pltpu.VMEM((ITERS, 4, N_Y, N_Z, 2, STRIPE, ROWS), BF16),
            pltpu.VMEM((2, 2 * COLS, ROWS), BF16),
            pltpu.VMEM((2, 2 * COLS, ROWS), BF16),
            pltpu.VMEM((2 * COLS, ROWS), F32),
            pltpu.VMEM((2 * COLS, ROWS), F32),
            pltpu.VMEM((STRIPE, ROWS), F32),
            pltpu.VMEM((128, 128), F32),
            dma((ITERS, len(PIECES))),
            dma((ITERS, len(PIECES))),
            dma((ITERS, 3)),
            dma((ITERS, 3)),
            dma((ITERS, 3)),
            dma((ITERS, 3)),
            dma((ITERS,)),
            dma((ITERS, 2, 26)),
            dma((2,)),
        ],
        compiler_params=pltpu.CompilerParams(
            collective_id=0, has_side_effects=True, vmem_limit_bytes=53 * 2**20 + 2**18
        ),
        cost_estimate=pl.CostEstimate(
            flops=ITERS * 8 * COLS * 1536 * ROWS, bytes_accessed=4 * 2**20, transcendentals=0
        ),
    )(green.reshape(2, COLS, ROWS), jnp.stack([hamiltonian, interaction]))
    return result.reshape(shape)


def solution(mesh):
    in_specs = (P(None, None, "tp", None, "ta"), P(), P())
    out_specs = P(None, None, "tp", None, "ta")
    return jax.shard_map(shards, mesh=mesh, in_specs=in_specs, out_specs=out_specs, check_vma=False)
```

```python
import functools

import jax
import jax.numpy as jnp
from jax import lax
from jax.experimental import pallas as pl
from jax.experimental.pallas import tpu as pltpu
from jax.sharding import PartitionSpec as P

NO = 32
ITERS = 2
N_TA = 8
N_TP = 32
N_Y = 4
N_Z = 4
STRIPE = 16
ROWS = 512
COLS = 128
FACTOR = 1.0 / 32.0
PIECES = ((1, 2, 0, 256), (0, 1, 0, 128), (5, 1, 128, 128))

MESH = pl.DeviceIdType.MESH
HIGHEST = lax.Precision.HIGHEST
F32 = jnp.float32
BF16 = jnp.bfloat16


def iota(shape, dim):
    return lax.broadcasted_iota(jnp.int32, shape, dim)


def exact_dot(left, right, contract=((1,), (0,))):
    return lax.dot_general(
        left, right, (contract, ((), ())), precision=HIGHEST, preferred_element_type=F32
    )


def kernel(
    green_hbm,
    orbital_hbm,
    out_ref,
    green_ref,
    orbital_ref,
    rounded,
    previous,
    earliest,
    stage_out,
    stage_in,
    mirror_out,
    mirror_in,
    flipped,
    window,
    straight,
    crossed,
    total,
    hamilton,
    weights,
    blocked,
    row_send,
    row_recv,
    stage_send,
    stage_recv,
    mirror_send,
    mirror_recv,
    window_send,
    window_recv,
    input_sem,
):
    ta = lax.axis_index("ta")
    tp = lax.axis_index("tp")
    y = tp // 8
    zl = lax.rem(tp // 2, 4)
    core = lax.rem(tp, 2)

    def ta_plus(k):
        return lax.rem(ta + k + N_TA, N_TA)

    near = zl + 1 - 2 * lax.rem(zl, 2)
    middle = 2 - zl // 2
    far = 3 * (1 - zl // 2)
    z_order = (zl, near, middle, far)

    def stripe_of(q):
        return pl.ds(pl.multiple_of(q * STRIPE, STRIPE), STRIPE)

    def place(dy, z, c):
        return lax.rem(y + dy, N_Y) * 8 + z * 2 + c

    inputs = [
        pltpu.make_async_copy(src, dst, input_sem.at[n])
        for n, (src, dst) in enumerate(
            ((green_hbm, green_ref), (orbital_hbm, orbital_ref))
        )
    ]
    for copy in inputs:
        copy.start()

    barrier = pltpu.get_barrier_semaphore()

    for dy in (1, 2, 3):
        pl.semaphore_signal(
            barrier, inc=1, device_id=(ta, place(dy, zl, core)), device_id_type=MESH
        )
    for k in (1, 2, 0):
        for z in (far, middle, near, zl):
            for other in (1, 0):
                if k == 0 and z is zl and other == 0:
                    continue
                c = 1 - core if other else core
                pl.semaphore_signal(
                    barrier,
                    inc=1,
                    device_id=(ta_plus(-k), place(0, z, c)),
                    device_id_type=MESH,
                )

    def remote(src, dst, send, recv, target):
        return pltpu.make_async_remote_copy(
            src_ref=src,
            dst_ref=dst,
            send_sem=send,
            recv_sem=recv,
            device_id=target,
            device_id_type=MESH,
        )

    def build_stage(state, it):
        for k in range(3):
            group = pl.multiple_of(ta_plus(k) * STRIPE, STRIPE)
            for r in range(2):
                piece = state[r, pl.ds(group, STRIPE), :].astype(BF16)
                for j in range(N_Y):
                    stage_out[it, j, pl.ds((2 * k + r) * STRIPE, STRIPE), :] = piece[
                        :, j * 128 : (j + 1) * 128
                    ]

    def build_rounded(state, it):
        for r in range(2):
            rounded[it, pl.ds(r * COLS, COLS), :] = state[r].astype(BF16)

    def row_copy(it, n):
        k, start, count = PIECES[n][1:]
        return remote(
            rounded.at[it, pl.ds(start, count)],
            (previous if k == 1 else earliest).at[it, pl.ds(start, count)],
            row_send.at[it, n],
            row_recv.at[it, n],
            (ta_plus(k), tp),
        )

    def stage_copy(it, dy):
        j = lax.rem(y + dy, N_Y)
        return remote(
            stage_out.at[it, j],
            stage_in.at[it, y],
            stage_send.at[it, dy - 1],
            stage_recv.at[it, dy - 1],
            (ta, place(dy, zl, core)),
        )

    def build_mirror(it):
        stage_in[it, y] = stage_out[it, y]
        for k in (1, 2, 0):
            stacked = jnp.concatenate(
                [stage_in[it, j, pl.ds(2 * k * STRIPE, 2 * STRIPE), :] for j in range(N_Y)],
                axis=0,
            )
            mirror_out[it, k] = stacked.astype(F32).T.astype(BF16)
            send_mirror(it, k)
        own = stripe_of(zl * 2 + core)
        mirror_in[it, 0, own, :] = mirror_out[it, 0, own, :]

    def send_mirror(it, k):
        for z in (far, middle, near, zl):
            for other in (1, 0):
                if k == 0 and z is zl and other == 0:
                    continue
                c = 1 - core if other else core
                remote(
                    mirror_out.at[it, k, stripe_of(z * 2 + c), :],
                    mirror_in.at[it, k, stripe_of(zl * 2 + core), :],
                    mirror_send.at[it, k],
                    mirror_recv.at[it, k],
                    (ta_plus(k), place(0, z, c)),
                ).start()

    def mirror_bytes(ref, it, k):
        return ref.at[it, k] if k else ref.at[it, 0, pl.ds(0, 7 * STRIPE), :]

    def wait_bytes(ref, sem):
        pltpu.make_async_copy(ref, ref, sem).wait()

    def flip(it, k):
        piece = iota((STRIPE, 128), 1) // STRIPE
        parts = [
            mirror_in[it, k, pl.ds(i * STRIPE, STRIPE), :].astype(F32) for i in range(8)
        ]
        for bit in (1, 2, 4):
            low = (piece // bit) % 2 == 0
            for i in range(8):
                if i & bit:
                    continue
                first, second = parts[i], parts[i | bit]
                parts[i] = jnp.where(low, first, pltpu.roll(second, STRIPE * bit, 1))
                parts[i | bit] = jnp.where(
                    low, pltpu.roll(first, 128 - STRIPE * bit, 1), second
                )
        for j in range(N_Y):
            for r in range(2):
                flipped[k, r, :, pl.ds(j * 128, 128)] = parts[2 * j + r]

    def column(state, r, k):
        group = pl.multiple_of(ta_plus(-k) * STRIPE, STRIPE)
        return state[r, pl.ds(group, STRIPE), :]

    def self_energy(it, kind, real, imag, mirror_real, mirror_imag):
        real_square = real * real - imag * imag
        imag_square = 2.0 * real * imag
        coupling = weights[...]
        window[it, 2 * kind, y, zl, core] = (
            coupling * (real_square * mirror_real - imag_square * mirror_imag)
        ).astype(BF16)
        window[it, 2 * kind + 1, y, zl, core] = (
            coupling * (real_square * mirror_imag + imag_square * mirror_real)
        ).astype(BF16)

    def sigma_combined(state, it):
        later = iota((STRIPE, ROWS), 1) // NO < tp // 2
        real, imag = (
            jnp.where(later, column(state, r, 2), column(state, r, 0)) for r in range(2)
        )
        mirror_real, mirror_imag = (
            jnp.where(later, flipped[2, r], flipped[0, r]) for r in range(2)
        )
        self_energy(it, 0, real, imag, mirror_real, mirror_imag)

    def sigma_middle(state, it):
        self_energy(
            it, 1, column(state, 0, 1), column(state, 1, 1), flipped[1, 0], flipped[1, 1]
        )

    def send_own(it, kind):
        part = window.at[it, pl.ds(2 * kind, 2), y, :, core]
        for z in (near, middle, far):
            remote(
                part.at[:, zl],
                part.at[:, zl],
                window_send.at[it],
                window_recv.at[it, kind, zl],
                (ta, place(0, z, core)),
            ).start()

    def wait_z(it, kind, z):
        part = window.at[it, pl.ds(2 * kind, 2), y, :, core]
        wait_bytes(part.at[:, z], window_recv.at[it, kind, z])

    def y_part(it, kind, dy, piece):
        part = window.at[it, pl.ds(2 * kind, 2), lax.rem(y + dy, N_Y)]
        return part.at[:, z_order[piece], core]

    def y_copy(it, kind, piece, source, target):
        part = y_part(it, kind, source, piece)
        return remote(
            part,
            part,
            window_send.at[it],
            window_recv.at[it, kind, 4 + 4 * piece + lax.rem(y + source, N_Y)],
            (ta, place(target, zl, core)),
        )

    def send_y(it, kind, piece):
        for dy in (2, 1, 3) if piece == 3 else (1, 3):
            y_copy(it, kind, piece, 0, dy).start()

    def wait_y(it, kind, piece, dy):
        wait_bytes(
            y_part(it, kind, dy, piece),
            window_recv.at[it, kind, 4 + 4 * piece + lax.rem(y + dy, N_Y)],
        )

    def relay(it, kind, piece):
        source, target = ((3, 1), (1, 3))[kind]
        wait_y(it, kind, piece, source)
        y_copy(it, kind, piece, source, target).start()

    def send_sibling(it, kind, dy):
        j = lax.rem(y + dy, N_Y)
        part = window.at[it, pl.ds(2 * kind, 2), j, :, core]
        remote(
            part,
            part,
            window_send.at[it],
            window_recv.at[it, kind, 20 + j],
            (ta, place(0, zl, 1 - core)),
        ).start()

    def wait_sibling(it, kind, dy):
        j = lax.rem(y + dy, N_Y)
        wait_bytes(
            window.at[it, pl.ds(2 * kind, 2), j, :, 1 - core], window_recv.at[it, kind, 20 + j]
        )

    def last_part(it, kind, pair, c):
        j = lax.rem(y + 2, N_Y)
        return window.at[it, pl.ds(2 * kind, 2), j, pl.ds(2 * pair, 2), c]

    def pass_last(it, kind):
        for half in range(2):
            pair = zl // 2 if half == 0 else 1 - zl // 2
            for piece in (2 * half, 2 * half + 1):
                wait_y(it, kind, piece, 2)
            part = last_part(it, kind, pair, core)
            remote(
                part,
                part,
                window_send.at[it],
                window_recv.at[it, kind, 24 + half],
                (ta, place(0, zl, 1 - core)),
            ).start()

    def wait_last(it, kind):
        for half in range(2):
            pair = zl // 2 if half == 0 else 1 - zl // 2
            wait_bytes(last_part(it, kind, pair, 1 - core), window_recv.at[it, kind, 24 + half])

    def lefts(it, which, source, keep):
        for r in range(2):
            half = source[it, pl.ds(r * COLS, COLS), :]
            if keep is not None:
                half = jnp.where(keep, half, jnp.zeros_like(half))
            straight[which, pl.ds(r * COLS, COLS), :] = half
            crossed[which, pl.ds((1 - r) * COLS, COLS), :] = -half if r == 1 else half

    def rows_of(it, part, j):
        return window[it, part, j].reshape(128, ROWS)

    def multiply_combined(it, dy):
        j = lax.rem(y + dy, N_Y)
        lanes = pl.ds(pl.multiple_of(j * 128, 128), 128)
        later = (j * 4 + iota((128, ROWS), 0) // NO) > iota((128, ROWS), 1) // NO
        old = jnp.where(later, 1.0, 0.0).astype(BF16)
        new = jnp.where(later, 0.0, 1.0).astype(BF16)
        left_parts, right_parts = [], []
        for r, side in ((0, straight), (1, crossed)):
            combined = rows_of(it, r, j)
            right_parts += [combined * new, combined * old]
            left_parts += [side[which, :, lanes] for which in range(2)]
        product = jnp.dot(
            jnp.concatenate(left_parts, axis=1),
            jnp.concatenate(right_parts, axis=0),
            preferred_element_type=F32,
        )
        if dy == 0:
            total[...] = product
        else:
            total[...] += product

    def multiply_middle(it, r):
        left = previous[it, pl.ds(r * COLS, COLS), :]
        left = jnp.where(ta >= 1, left, jnp.zeros_like(left))
        with_real, with_imag = (
            jnp.dot(
                left, window[it, 2 + part].reshape(ROWS, ROWS), preferred_element_type=F32
            )
            for part in range(2)
        )
        top, bottom = pl.ds(0, COLS), pl.ds(COLS, COLS)
        if r == 0:
            total[top, :] += with_real
            total[bottom, :] += with_imag
        else:
            total[top, :] -= with_imag
            total[bottom, :] += with_real

    def hamilton_term(state):
        for r in range(2):
            for b in range(4):
                lanes = pl.ds(b * 128, 128)
                hamilton[pl.ds(r * COLS, COLS), lanes] = exact_dot(
                    state[r, :, lanes], blocked[...]
                )

    def prepare():
        squared = orbital_ref[1] * orbital_ref[1]
        pick = (iota((STRIPE, NO), 1) == core * STRIPE + iota((STRIPE, NO), 0)).astype(F32)
        picked = exact_dot(pick, squared, ((1,), (1,)))
        spread = (lax.rem(iota((NO, ROWS), 1), NO) == iota((NO, ROWS), 0)).astype(F32)
        weights[...] = exact_dot(picked, spread)
        tall = (lax.rem(iota((128, NO), 0), NO) == iota((128, NO), 1)).astype(F32)
        wide = (lax.rem(iota((NO, 128), 1), NO) == iota((NO, 128), 0)).astype(F32)
        across = exact_dot(exact_dot(tall, orbital_ref[0], ((1,), (1,))), wide)
        same = iota((128, 128), 0) // NO == iota((128, 128), 1) // NO
        blocked[...] = jnp.where(same, across, 0.0)

    for copy in inputs:
        copy.wait()
    build_stage(green_ref, 0)
    pl.semaphore_wait(barrier, 26)

    started = []
    for it in range(ITERS):
        state = green_ref if it == 0 else out_ref
        if it:
            build_stage(state, it)
        stages = [stage_copy(it, dy) for dy in (1, 2, 3)]
        for n in (1, 0, 2):
            stages[n].start()
        build_rounded(state, it)
        rows = [row_copy(it, n) for n in range(len(PIECES))]

        def start_rows(stage):
            for piece, copy in zip(PIECES, rows):
                if piece[0] == stage:
                    copy.start()

        def wait_rows(k):
            for piece, copy in zip(PIECES, rows):
                if piece[1] == k:
                    copy.wait_recv()

        start_rows(0)
        if it == 0:
            prepare()
        lefts(it, 0, rounded, None)
        hamilton_term(state)
        for copy in stages:
            copy.wait_recv()
        build_mirror(it)
        start_rows(1)
        for k in (0, 2):
            wait_bytes(mirror_bytes(mirror_in, it, k), mirror_recv.at[it, k])
            flip(it, k)
        sigma_combined(state, it)
        send_own(it, 0)
        send_y(it, 0, 0)
        start_rows(3)
        wait_bytes(mirror_bytes(mirror_in, it, 1), mirror_recv.at[it, 1])
        flip(it, 1)
        sigma_middle(state, it)
        send_own(it, 1)
        send_y(it, 1, 0)
        start_rows(4)
        for kind in range(2):
            wait_z(it, kind, near)
            send_y(it, kind, 1)
        for kind in range(2):
            relay(it, kind, 0)
        for kind in range(2):
            wait_z(it, kind, middle)
            send_y(it, kind, 2)
        for kind in range(2):
            relay(it, kind, 1)
        for kind in range(2):
            wait_z(it, kind, far)
            send_y(it, kind, 3)
            send_sibling(it, kind, 0)
        start_rows(5)
        for kind in range(2):
            relay(it, kind, 2)
        for kind in range(2):
            dy = 3 if kind == 0 else 1
            wait_y(it, kind, 3, dy)
            send_sibling(it, kind, dy)
        for kind in range(2):
            dy = 1 if kind == 0 else 3
            for piece in range(4):
                wait_y(it, kind, piece, dy)
            send_sibling(it, kind, dy)
        wait_rows(2)
        lefts(it, 1, earliest, ta >= 2)
        wait_sibling(it, 0, 0)
        multiply_combined(it, 0)
        pass_last(it, 0)
        for dy in (3, 1):
            wait_sibling(it, 0, dy)
            multiply_combined(it, dy)
        pass_last(it, 1)
        wait_last(it, 0)
        multiply_combined(it, 2)
        for dy in (0, 1, 3):
            wait_sibling(it, 1, dy)
        wait_last(it, 1)
        for r in range(2):
            rows[1 + r].wait_recv()
            multiply_middle(it, r)
        out_real = state[0] + 0.5 * (
            hamilton[pl.ds(COLS, COLS), :] + FACTOR * total[pl.ds(COLS, COLS), :]
        )
        out_imag = state[1] - 0.5 * (
            hamilton[pl.ds(0, COLS), :] + FACTOR * total[pl.ds(0, COLS), :]
        )
        out_ref[0] = out_real
        out_ref[1] = out_imag
        started.append(rows + stages)

    for it in range(ITERS):
        for k in range(3):
            wait_bytes(mirror_bytes(mirror_out, it, k), mirror_send.at[it, k])
        for copy in started[it]:
            copy.wait_send()
        wait_bytes(window.at[it, :, pl.ds(0, 3)], window_send.at[it])
        wait_bytes(window.at[it, :, 3, pl.ds(0, 3)], window_send.at[it])
        wait_bytes(window.at[it, :, 3, 3, 0], window_send.at[it])


def shards(green, hamiltonian, interaction):
    shape = green.shape
    whole = pl.BlockSpec(memory_space=pltpu.VMEM)
    dma = pltpu.SemaphoreType.DMA
    result = pl.pallas_call(
        kernel,
        out_shape=jax.ShapeDtypeStruct((2, COLS, ROWS), F32),
        in_specs=[pl.BlockSpec(memory_space=pltpu.HBM)] * 2,
        out_specs=whole,
        scratch_shapes=[
            pltpu.VMEM((2, COLS, ROWS), F32),
            pltpu.VMEM((2, NO, NO), F32),
            pltpu.VMEM((ITERS, 2 * COLS, ROWS), BF16),
            pltpu.VMEM((ITERS, 2 * COLS, ROWS), BF16),
            pltpu.VMEM((ITERS, 2 * COLS, ROWS), BF16),
            pltpu.VMEM((ITERS, N_Y, 6 * STRIPE, 128), BF16),
            pltpu.VMEM((ITERS, N_Y, 6 * STRIPE, 128), BF16),
            pltpu.VMEM((ITERS, 3, 128, 128), BF16),
            pltpu.VMEM((ITERS, 3, 128, 128), BF16),
            pltpu.VMEM((3, 2, STRIPE, ROWS), F32),
            pltpu.VMEM((ITERS, 4, N_Y, N_Z, 2, STRIPE, ROWS), BF16),
            pltpu.VMEM((2, 2 * COLS, ROWS), BF16),
            pltpu.VMEM((2, 2 * COLS, ROWS), BF16),
            pltpu.VMEM((2 * COLS, ROWS), F32),
            pltpu.VMEM((2 * COLS, ROWS), F32),
            pltpu.VMEM((STRIPE, ROWS), F32),
            pltpu.VMEM((128, 128), F32),
            dma((ITERS, len(PIECES))),
            dma((ITERS, len(PIECES))),
            dma((ITERS, 3)),
            dma((ITERS, 3)),
            dma((ITERS, 3)),
            dma((ITERS, 3)),
            dma((ITERS,)),
            dma((ITERS, 2, 26)),
            dma((2,)),
        ],
        compiler_params=pltpu.CompilerParams(
            collective_id=0, has_side_effects=True, vmem_limit_bytes=53 * 2**20 + 2**18
        ),
        cost_estimate=pl.CostEstimate(
            flops=ITERS * 8 * COLS * 1536 * ROWS, bytes_accessed=4 * 2**20, transcendentals=0
        ),
    )(green.reshape(2, COLS, ROWS), jnp.stack([hamiltonian, interaction]))
    return result.reshape(shape)


def solution(mesh):
    in_specs = (P(None, None, "tp", None, "ta"), P(), P())
    out_specs = P(None, None, "tp", None, "ta")
    return jax.shard_map(shards, mesh=mesh, in_specs=in_specs, out_specs=out_specs, check_vma=False)
```
